256 devices in a mesh: section: 8 (over z), dp: 32 (over x, y, core).
Axes of the slice: x: 4, y: 4, z: 8, core: 2. Of those that a mesh axis runs over, the one named last changes fastest.
Arguments:
- x0: bfloat16 [4, 1024, 5120], P(None, 'dp'), may hold values from -6 to 6
- w_key: bfloat16 [8, 5120, 512], P('section'), may hold values from -0.078125 to 0.078125
- w_value: bfloat16 [8, 5120, 512], P('section'), may hold values from -0.078125 to 0.078125
- w_score: float32 [5120], replicated, may hold values from -0.078125 to 0.078125
- segments: int32 [4, 1024], P(None, 'dp'), may hold values from 0 to 31, as said below
- lengths: int32 [4, 32], P(None, 'dp'), may hold values from 1 to 32, as said below
- grades: int32 [4, 1024], P(None, 'dp'), may hold values from 0 to 3
Outputs:
- grad_key: float32 [8, 5120, 512], P('section', 'dp')
- grad_value: float32 [8, 5120, 512], P('section', 'dp')
The draws below stay inside these ranges and needn't reach their ends.
Inputs may be any that keep to these rules, and one draw needn't show every extreme that they name: `segments`: within each packed row of 32 slots the ids start at 0 and never fall; in every draw some packed row has a new id at every slot. `lengths`: every packed row has its live tokens at the front; in every draw some packed row is full.
All inputs are finite; a program needn't handle non-finite values.
Results may differ from the reference program's by a relative error of at most 0.035.
Values may be sent and summed in bfloat16 or wider, within the bound.
A program may use at most 128 MiB of HBM per device.

```python
import jax
import jax.numpy as jnp
from jax import lax

D = 5120
HD = 128
KV_HEADS = 4
ROWS = 32
MICRO = 4
KW = 512
LAYERS = 8
TOKENS = 1024
N_DP = 32


def draw_segments(key, part):
    key = jax.random.fold_in(key, 11)
    first_key, second_key = jax.random.split(key)
    count = MICRO * (TOKENS // ROWS)
    starts = jax.random.randint(first_key, (count, ROWS), 0, 12) == 0
    index = jnp.arange(ROWS, dtype=jnp.int32)
    chosen = jax.random.randint(second_key, (), 0, count)
    starts = starts | (index == 0)[None, :] | (jnp.arange(count, dtype=jnp.int32) == chosen)[:, None]
    ident = jnp.cumsum(starts.astype(jnp.int32), axis=-1) - 1
    return ident.reshape(MICRO, TOKENS).astype(jnp.int32)


def draw_lengths(key, part):
    key = jax.random.fold_in(key, 23)
    first_key, second_key = jax.random.split(key)
    count = MICRO * (TOKENS // ROWS)
    divisor = jax.random.randint(first_key, (count,), 1, 8)
    live = ROWS // divisor
    chosen = jax.random.randint(second_key, (), 0, count)
    live = jnp.where(jnp.arange(count, dtype=jnp.int32) == chosen, ROWS, live)
    return live.reshape(MICRO, TOKENS // ROWS).astype(jnp.int32)


def with_ends(values, stream_key, smallest, high):
    longest = values.shape.index(max(values.shape))
    spots = []
    for shift in (0, 1):
        where = [jax.random.randint(jax.random.fold_in(stream_key, axis), (), 0, length) for axis, length in enumerate(values.shape)]
        where[longest] = (where[longest] + shift) % values.shape[longest]
        spots.append(tuple(where))
    return values.at[spots[0]].set(smallest).at[spots[1]].set(high)


def level_of(rng, dims, cuts, least, largest):
    def one(position, parts):
        heights = jax.random.uniform(jax.random.fold_in(jax.random.fold_in(rng, 6), position), (parts,), jnp.float32, least / len(cuts), largest / len(cuts))
        return jnp.repeat(jnp.exp(heights), dims[position] // parts).reshape((-1,) + (1,) * (len(dims) - position - 1))

    factor_of = one(*cuts[0])
    for cut in cuts[1:]:
        factor_of = factor_of * one(*cut)
    return factor_of


def centred(own_key, extent, scale, reach, shards=(), kind=jnp.bfloat16):
    result = jax.random.normal(own_key, extent, jnp.float32) * scale
    if len(shards) > 0:
        result = level_of(own_key, extent, shards, -0.22, 0.18) * result
    return jnp.clip(result, min=-reach, max=reach).astype(kind)


def setup_inputs(seed: int = 0) -> dict:
    keys = jax.random.split(jax.random.key(seed), 8)
    return {
        "x0": centred(keys[0], (MICRO, TOKENS, D), 1.0, 6.0, ((1, 32),)),
        "w_key": centred(keys[1], (LAYERS, D, KW), D ** -0.5, 0.078125, ((0, 8),)),
        "w_value": centred(keys[2], (LAYERS, D, KW), D ** -0.5, 0.078125, ((0, 8),)),
        "w_score": centred(keys[3], (D,), D ** -0.5, 0.078125, (), jnp.float32),
        "segments": draw_segments(jax.random.fold_in(keys[7], 71), 0),
        "lengths": draw_lengths(jax.random.fold_in(keys[7], 71), 0),
        "grades": with_ends(jax.random.randint(keys[6], (MICRO, TOKENS), 0, 4), jax.random.fold_in(keys[6], 1), 0, 3).astype(jnp.int32),
    }


EPS = 1e-06
THETA = 1000000.0

def matmul(left, right):
    flat = left.reshape(-1, left.shape[-1])
    return jnp.dot(flat, right, preferred_element_type=jnp.float32).reshape(left.shape[:-1] + (right.shape[-1],))

def rope_tables(segments):
    width = segments.shape[-1]
    index = jnp.arange(width, dtype=jnp.int32)
    section_begin_offsets = jnp.concatenate([jnp.ones(segments.shape[:-1] + (1,), bool), segments[..., 1:] != segments[..., :-1]], axis=-1)
    leading_half = lax.cummax(jnp.where(section_begin_offsets, index, jnp.int32(0)), axis=segments.ndim - 1)
    offset = (index - leading_half).astype(jnp.float32)
    freqs = THETA ** (-(jnp.arange(HD // 2, dtype=jnp.float32) * 2.0) / HD)
    angles = offset[..., None] * freqs
    return (jnp.cos(angles), jnp.sin(angles))

def allowed_mask(segments, lengths):
    width = segments.shape[-1]
    index = jnp.arange(width, dtype=jnp.int32)
    same = segments[..., :, None] == segments[..., None, :]
    causal = index[None, :] <= index[:, None]
    live = index < lengths
    allowed = same & causal & live[..., :, None] & live[..., None, :]
    return allowed | jnp.eye(width, dtype=bool)

def rotate(vectors, cosine, sine_table):
    half = HD // 2
    cosine_value = cosine[..., :, None, :]
    sine_value = sine_table[..., :, None, :]
    leading_half, trailing_half = (vectors[..., :half], vectors[..., half:])
    return jnp.concatenate([leading_half * cosine_value - trailing_half * sine_value, trailing_half * cosine_value + leading_half * sine_value], axis=-1)

def rotate_back(grads, cosine, sine_table):
    half = HD // 2
    cosine_value = cosine[..., :, None, :]
    sine_value = sine_table[..., :, None, :]
    leading_half, trailing_half = (grads[..., :half], grads[..., half:])
    return jnp.concatenate([leading_half * cosine_value + trailing_half * sine_value, trailing_half * cosine_value - leading_half * sine_value], axis=-1)

def normalize(hidden):
    hfull = hidden.astype(jnp.float32)
    scale = lax.rsqrt(lax.optimization_barrier(jnp.mean(hfull * hfull, axis=-1, keepdims=True)) + EPS)
    return (hfull, scale)

def heads(array):
    return array.reshape(array.shape[:-1] + (KV_HEADS, HD))

def attend(keys_b, values_b, allowed):
    kf = keys_b.astype(jnp.float32)
    scores = jnp.einsum('...ihd,...jhd->...hij', kf, kf) / HD
    scores = jnp.where(allowed[..., None, :, :], scores, -1e+30)
    probs = jax.nn.softmax(scores, axis=-1)
    probs_b = probs.astype(jnp.bfloat16)
    mixed = jnp.einsum('...hij,...jhd->...ihd', probs_b.astype(jnp.float32), values_b.astype(jnp.float32))
    return (probs, probs_b, mixed)

def layer_forward(hidden, w_key, w_value, cosine, sine_table, allowed):
    hfull, scale = normalize(hidden)
    normed = (hfull * scale).astype(jnp.bfloat16)
    keys_b = rotate(heads(matmul(normed, w_key)), cosine, sine_table).astype(jnp.bfloat16)
    values_b = heads(matmul(normed, w_value).astype(jnp.bfloat16))
    probs, probs_b, mixed = attend(keys_b, values_b, allowed)
    mixed_b = mixed.astype(jnp.bfloat16).reshape(hidden.shape[:-1] + (KW,))
    output = hfull + matmul(mixed_b, w_value.T)
    return (output.astype(jnp.bfloat16), keys_b, values_b)

def layer_backward(hidden, keys_b, values_b, grad_out, w_key, w_value, cosine, sine_table, allowed):
    hfull, scale = normalize(hidden)
    probs, probs_b, mixed = attend(keys_b, values_b, allowed)
    mixed_b = mixed.astype(jnp.bfloat16).reshape(hidden.shape[:-1] + (KW,))
    grad_mixed = heads(matmul(grad_out, w_value).astype(jnp.bfloat16)).astype(jnp.float32)
    grad_probs = jnp.einsum('...ihd,...jhd->...hij', grad_mixed, values_b.astype(jnp.float32))
    grad_values = jnp.einsum('...hij,...ihd->...jhd', probs_b.astype(jnp.float32), grad_mixed)
    grad_values = grad_values.astype(jnp.bfloat16).reshape(hidden.shape[:-1] + (KW,))
    grad_scores = (probs * (grad_probs - lax.optimization_barrier(jnp.sum(probs * grad_probs, axis=-1, keepdims=True)))).astype(jnp.bfloat16)
    gsf = grad_scores.astype(jnp.float32)
    kf = keys_b.astype(jnp.float32)
    grad_keys = (jnp.einsum('...hij,...jhd->...ihd', gsf, kf) + jnp.einsum('...hij,...ihd->...jhd', gsf, kf)) / HD
    grad_keys = rotate_back(grad_keys, cosine, sine_table).astype(jnp.bfloat16).reshape(hidden.shape[:-1] + (KW,))
    grad_normed = matmul(grad_keys, w_key.T) + matmul(grad_values, w_value.T)
    incoming_gradient = grad_out.astype(jnp.float32) + scale * grad_normed - hfull * scale ** 3 * lax.optimization_barrier(jnp.mean(grad_normed * hfull, axis=-1, keepdims=True))
    normed = (hfull * scale).astype(jnp.bfloat16)
    return (incoming_gradient.astype(jnp.bfloat16), normed, grad_keys, grad_values, mixed_b)

def loss_gradient(hidden, segments, length, grades, w_score):
    hfull, scale = normalize(hidden)
    xfull = hfull * scale
    score = jnp.dot(xfull, w_score, precision=lax.Precision.HIGHEST)
    width = segments.shape[-1]
    index = jnp.arange(width, dtype=jnp.int32)
    following = jnp.concatenate([segments[..., 1:] != segments[..., :-1], jnp.ones(segments.shape[:-1] + (1,), bool)], axis=-1)
    ends = (index < length) & (following | (index == length - 1))
    target = jax.nn.softmax(jnp.where(ends, grades.astype(jnp.float32), -1e+30), axis=-1)
    model = jax.nn.softmax(jnp.where(ends, score, -1e+30), axis=-1)
    weight = jnp.where(ends, model - target, 0.0)
    grad_x = weight[..., None] * w_score
    grad_h = scale * grad_x - hfull * scale ** 3 * lax.optimization_barrier(jnp.mean(grad_x * hfull, axis=-1, keepdims=True))
    return grad_h.astype(jnp.bfloat16)

def reference(x0, w_key, w_value, w_score, segments, lengths, grades):
    row_segments = segments.reshape(MICRO, N_DP, ROWS)
    row_lengths = lengths[..., None]
    row_grades = grades.reshape(MICRO, N_DP, ROWS)
    cosine, sine_table = rope_tables(row_segments)
    allowed = allowed_mask(row_segments, row_lengths)
    hidden = x0.reshape(MICRO, N_DP, ROWS, D)
    saved = []
    for layer in range(LAYERS):
        produced, keys_b, values_b = layer_forward(hidden, w_key[layer], w_value[layer], cosine, sine_table, allowed)
        saved.append((hidden, keys_b, values_b))
        hidden = produced
    grad = loss_gradient(hidden, row_segments, row_lengths, row_grades, w_score)
    key_list = []
    value_list = []
    for layer in range(LAYERS - 1, -1, -1):
        h_in, keys_b, values_b = saved[layer]
        incoming_gradient, normed, grad_keys, grad_values, mixed_b = layer_backward(h_in, keys_b, values_b, grad, w_key[layer], w_value[layer], cosine, sine_table, allowed)
        normed2 = normed.reshape(-1, D)
        grad2 = grad.reshape(-1, D)
        key_list.append(jnp.dot(normed2.T, grad_keys.reshape(-1, KW), preferred_element_type=jnp.float32))
        value_list.append(jnp.dot(normed2.T, grad_values.reshape(-1, KW), preferred_element_type=jnp.float32) + jnp.dot(grad2.T, mixed_b.reshape(-1, KW), preferred_element_type=jnp.float32))
        grad = incoming_gradient
    grad_key = jnp.stack(key_list[::-1], axis=0)
    grad_value = jnp.stack(value_list[::-1], axis=0)
    return (grad_key, grad_value)
```

```python
import functools

import jax
import jax.numpy as jnp
from jax import lax
from jax.experimental import pallas as pl
from jax.experimental.pallas import tpu as pltpu
from jax.sharding import PartitionSpec as P

HD = 128
HEADS = 4
EPS = 1e-06
THETA = 1000000.0
SUB = 16
PIECES = 4
MESH = pl.DeviceIdType.MESH
F32 = jnp.float32
BF16 = jnp.bfloat16


def dot(left, right):
    return jnp.dot(left, right, preferred_element_type=F32)


def dot_t(left, right):
    return lax.dot_general(left, right, (((1,), (1,)), ((), ())), preferred_element_type=F32)


def t_dot(left, right):
    return lax.dot_general(left, right, (((0,), (0,)), ((), ())), preferred_element_type=F32)


def stack(array):
    return jnp.concatenate([array[:, h * HD : (h + 1) * HD] for h in range(HEADS)], axis=0)


def unstack(array):
    return jnp.concatenate([array[h * SUB : (h + 1) * SUB] for h in range(HEADS)], axis=1)


def swap(array):
    return pltpu.roll(array, HD // 2, 1)


def tall(array):
    return jnp.concatenate([array] * HEADS, axis=0)


def pipe_kernel(
    sections,
    x0,
    wk,
    wv,
    wscore,
    cosine,
    sine,
    mask,
    ends,
    target,
    hin,
    gin,
    gks,
    gvs,
    mixs,
    hout,
    gout,
    keys,
    values,
    probs,
    scales,
    scores,
    oscales,
    gweights,
    carry_v,
    carry_k,
    local_sem,
    hsend,
    hrecv,
    gsend,
    grecv,
):
    section = lax.axis_index("section")
    last = sections - 1
    chunks = hin.shape[0]
    model = hin.shape[2]
    piece = model // PIECES
    up = jnp.minimum(section + 1, last)
    down = jnp.maximum(section - 1, 0)

    barrier = pltpu.get_barrier_semaphore()

    @pl.when(section < last)
    def _():
        pl.semaphore_signal(barrier, inc=1, device_id={"section": up}, device_id_type=MESH)

    @pl.when(section > 0)
    def _():
        pl.semaphore_signal(barrier, inc=1, device_id={"section": down}, device_id_type=MESH)

    @pl.when(section == 0)
    def _():
        copy = pltpu.make_async_copy(x0, hin, local_sem)
        copy.start()
        copy.wait()

    keys[...] = jnp.zeros_like(keys)
    values[...] = jnp.zeros_like(values)

    @pl.when((section > 0) & (section < last))
    def _():
        pl.semaphore_wait(barrier, 2)

    @pl.when((section == 0) | (section == last))
    def _():
        pl.semaphore_wait(barrier, 1)

    def columns(p):
        return pl.ds(p * piece, piece)

    def h_copy(c, p):
        return pltpu.make_async_remote_copy(
            src_ref=hout.at[c, :, columns(p)],
            dst_ref=hin.at[c, :, columns(p)],
            send_sem=hsend.at[c, p],
            recv_sem=hrecv.at[c, p],
            device_id={"section": up},
            device_id_type=MESH,
        )

    def g_copy(c, p):
        return pltpu.make_async_remote_copy(
            src_ref=gout.at[c, :, columns(p)],
            dst_ref=gin.at[c, :, columns(p)],
            send_sem=gsend.at[c, p],
            recv_sem=grecv.at[c, p],
            device_id={"section": down},
            device_id_type=MESH,
        )

    def forward(c):
        row = c // 2
        acc_k = jnp.zeros((SUB, HEADS * HD), F32)
        acc_v = jnp.zeros((SUB, HEADS * HD), F32)
        square = jnp.zeros((SUB, 1), F32)
        for p in range(PIECES):

            @pl.when(section > 0)
            def _():
                h_copy(c, p).wait_recv()

            part = hin[c, :, columns(p)]
            acc_k += dot(part, wk[columns(p), :])
            acc_v += dot(part, wv[columns(p), :])
            full = part.astype(F32)
            square += jnp.sum(full * full, axis=1, keepdims=True)
        scale = lax.rsqrt(square / model + EPS)
        scales[c] = scale
        turned = stack(acc_k * scale)
        turned = turned * tall(cosine[c]) + swap(turned) * tall(sine[c])
        key = turned.astype(BF16)
        value = stack(acc_v * scale).astype(BF16)
        keys[c] = key
        values[c] = value
        all_keys = keys[pl.ds(row * 2, 2)].reshape(2 * HEADS * SUB, HD)
        all_values = values[pl.ds(row * 2, 2)].reshape(2 * HEADS * SUB, HD)
        logits = dot_t(key, all_keys) * (1.0 / HD)
        logits = jnp.where(mask[c] > 0.0, logits, -1e30)
        top = jnp.max(logits, axis=1, keepdims=True)
        expd = jnp.exp(logits - top)
        prob = expd / jnp.sum(expd, axis=1, keepdims=True)
        probs[c] = prob
        mixed = unstack(dot(prob.astype(BF16), all_values).astype(BF16))
        mixs[c] = mixed
        for p in range(PIECES):
            out = hin[c, :, columns(p)].astype(F32) + dot_t(mixed, wv[columns(p), :])
            hout[c, :, columns(p)] = out.astype(BF16)

            @pl.when(section < last)
            def _():
                h_copy(c, p).start()

        @pl.when(section == last)
        def _():
            square = jnp.zeros((SUB, 1), F32)
            score = jnp.zeros((SUB, 1), F32)
            for p in range(PIECES):
                full = hout[c, :, columns(p)].astype(F32)
                square += jnp.sum(full * full, axis=1, keepdims=True)
                score += jnp.sum(full * wscore[:, columns(p)], axis=1, keepdims=True)
            scale = lax.rsqrt(square / model + EPS)
            oscales[c] = scale
            scores[c] = score * scale

    def backward(j):
        row = j // 2
        half = 1 - lax.rem(j, 2)
        c = row * 2 + half

        @pl.when(section == last)
        def _():
            both = pl.ds(row * 2, 2)
            end = ends[both]
            score = scores[both]
            masked = jnp.where(end > 0.0, score, -1e30)
            top = jnp.max(jnp.max(masked, axis=0), axis=0, keepdims=True)
            expd = jnp.where(end > 0.0, jnp.exp(masked - top[None]), 0.0)
            total = jnp.sum(jnp.sum(expd, axis=0), axis=0, keepdims=True)
            gweights[...] = jnp.where(end > 0.0, expd / total[None] - target[both], 0.0)
            weight = gweights[half]
            scale = oscales[c]
            first = scale * weight
            second = scale * scale * weight * scores[c] * (1.0 / model)
            for p in range(PIECES):
                full = hout[c, :, columns(p)].astype(F32)
                gin[c, :, columns(p)] = (first * wscore[:, columns(p)] - second * full).astype(BF16)

        acc = jnp.zeros((SUB, HEADS * HD), F32)
        for p in range(PIECES):

            @pl.when(section < last)
            def _():
                g_copy(c, p).wait_recv()

            acc += dot(gin[c, :, columns(p)], wv[columns(p), :])
        scale = scales[c]
        grad_mixed = stack(acc).astype(BF16)
        all_keys = keys[pl.ds(row * 2, 2)].reshape(2 * HEADS * SUB, HD)
        all_values = values[pl.ds(row * 2, 2)].reshape(2 * HEADS * SUB, HD)
        key = keys[c]
        value = values[c]
        prob = probs[c]
        grad_probs = dot_t(grad_mixed, all_values)
        product = prob * grad_probs
        grad_scores = (product - prob * jnp.sum(product, axis=1, keepdims=True)).astype(BF16)
        from_v = t_dot(prob.astype(BF16), grad_mixed)
        from_k = t_dot(grad_scores, key)
        lower = HEADS * SUB
        second = half == 1
        own_v = jnp.where(second, from_v[lower:], from_v[:lower] + carry_v[...])
        own_k = jnp.where(second, from_k[lower:], from_k[:lower] + carry_k[...])
        carry_v[...] = from_v[:lower]
        carry_k[...] = from_k[:lower]
        turned = (dot(grad_scores, all_keys) + own_k) * (1.0 / HD)
        grad_value = own_v.astype(BF16)
        along = jnp.sum(turned * key.astype(F32) + own_v * value.astype(F32), axis=1, keepdims=True)
        along = along[:SUB] + along[SUB : 2 * SUB] + along[2 * SUB : 3 * SUB] + along[3 * SUB :]
        along = along * (scale * scale) * (1.0 / model)
        grad_key = (turned * tall(cosine[c]) - swap(turned) * tall(sine[c])).astype(BF16)
        flat_key = unstack(grad_key)
        flat_value = unstack(grad_value)
        gks[c] = (flat_key.astype(F32) * scale).astype(BF16)
        gvs[c] = (flat_value.astype(F32) * scale).astype(BF16)

        @pl.when(section > 0)
        def _():
            for p in range(PIECES):
                grad = dot_t(flat_key, wk[columns(p), :]) + dot_t(flat_value, wv[columns(p), :])
                out = (
                    gin[c, :, columns(p)].astype(F32)
                    + scale * grad
                    - along * hin[c, :, columns(p)].astype(F32)
                )
                gout[c, :, columns(p)] = out.astype(BF16)
                g_copy(c, p).start()

    lead = jnp.where(section == last, 1, jnp.where(section == last - 1, 5, chunks))

    def slot(i, unused):
        @pl.when(i < chunks)
        def _():
            forward(i)

        j = i - lead

        @pl.when((j >= 0) & (j < chunks))
        def _():
            backward(j)

        return unused

    lax.fori_loop(0, 2 * chunks, slot, 0)

    def drain(c, unused):
        for p in range(PIECES):

            @pl.when(section < last)
            def _():
                h_copy(c, p).wait_send()

            @pl.when(section > 0)
            def _():
                g_copy(c, p).wait_send()

        return unused

    lax.fori_loop(0, chunks, drain, 0)


def tables(segments, lengths, grades):
    micro, width = segments.shape
    index = jnp.arange(width, dtype=jnp.int32)
    change = segments[:, 1:] != segments[:, :-1]
    starts = jnp.concatenate([jnp.ones((micro, 1), bool), change], axis=1)
    same = segments[:, :, None] == segments[:, None, :]
    first = jnp.max(jnp.where(starts[:, None, :] & (index[None, :] <= index[:, None]), index, 0), axis=2)
    offset = (index - first).astype(F32)
    freqs = THETA ** (-(jnp.arange(HD // 2, dtype=F32) * 2.0) / HD)
    angles = offset[..., None] * freqs
    cosine, sine = jnp.cos(angles), jnp.sin(angles)
    chunks = micro * width // SUB
    cosine = jnp.concatenate([cosine, cosine], axis=-1).reshape(chunks, SUB, HD)
    sine = jnp.concatenate([-sine, sine], axis=-1).reshape(chunks, SUB, HD)
    live = index < lengths
    causal = index[None, :] <= index[:, None]
    allowed = same & causal & live[:, :, None] & live[:, None, :]
    allowed = allowed | jnp.eye(width, dtype=bool)
    halves = width // SUB
    allowed = allowed.reshape(micro, halves, 1, SUB, halves, 1, SUB)
    heads = jnp.eye(HEADS, dtype=bool).reshape(1, 1, HEADS, 1, 1, HEADS, 1)
    mask = (allowed & heads).astype(F32).reshape(chunks, HEADS * SUB, halves * HEADS * SUB)
    following = jnp.concatenate([change, jnp.ones((micro, 1), bool)], axis=1)
    ends = live & (following | (index == lengths - 1))
    target = jax.nn.softmax(jnp.where(ends, grades.astype(F32), -1e30), axis=-1)
    ends = ends.astype(F32).reshape(chunks, SUB, 1)
    target = target.reshape(chunks, SUB, 1)
    return cosine, sine, mask, ends, target


def over_tokens(left, right):
    return t_dot(left, right)


def shards(x0, w_key, w_value, w_score, segments, lengths, grades):
    sections = lax.axis_size("section")
    micro, width, model = x0.shape
    features = w_key.shape[2]
    chunks = micro * width // SUB
    cosine, sine, mask, ends, target = tables(segments, lengths, grades)
    vmem = pl.BlockSpec(memory_space=pltpu.VMEM)
    act = (chunks, SUB, model)
    flat = (chunks, SUB, features)
    stacked = (chunks, HEADS * SUB, HD)
    hin, gin, gks, gvs, mixs = pl.pallas_call(
        functools.partial(pipe_kernel, sections),
        out_shape=[jax.ShapeDtypeStruct(s, BF16) for s in (act, act, flat, flat, flat)],
        in_specs=[pl.BlockSpec(memory_space=pl.ANY)] + [vmem] * 8,
        out_specs=[vmem] * 5,
        scratch_shapes=[
            pltpu.VMEM(act, BF16),
            pltpu.VMEM(act, BF16),
            pltpu.VMEM(stacked, BF16),
            pltpu.VMEM(stacked, BF16),
            pltpu.VMEM((chunks, HEADS * SUB, 2 * HEADS * SUB), F32),
            pltpu.VMEM((chunks, SUB, 1), F32),
            pltpu.VMEM((chunks, SUB, 1), F32),
            pltpu.VMEM((chunks, SUB, 1), F32),
            pltpu.VMEM((2, SUB, 1), F32),
            pltpu.VMEM((HEADS * SUB, HD), F32),
            pltpu.VMEM((HEADS * SUB, HD), F32),
            pltpu.SemaphoreType.DMA,
            pltpu.SemaphoreType.DMA((chunks, PIECES)),
            pltpu.SemaphoreType.DMA((chunks, PIECES)),
            pltpu.SemaphoreType.DMA((chunks, PIECES)),
            pltpu.SemaphoreType.DMA((chunks, PIECES)),
        ],
        compiler_params=pltpu.CompilerParams(
            collective_id=0, has_side_effects=True, vmem_limit_bytes=48 * 2**20
        ),
    )(
        x0.reshape(act),
        w_key[0],
        w_value[0],
        w_score.reshape(1, model),
        cosine,
        sine,
        mask,
        ends,
        target,
    )
    tokens = micro * width
    hidden = hin.reshape(tokens, model)
    grads = gin.reshape(tokens, model)
    part_key = over_tokens(hidden, gks.reshape(tokens, features))
    part_value = over_tokens(hidden, gvs.reshape(tokens, features)) + over_tokens(
        grads, mixs.reshape(tokens, features)
    )
    summed = lax.psum_scatter(
        jnp.concatenate([part_key, part_value], axis=1).astype(BF16),
        "dp",
        scatter_dimension=0,
        tiled=True,
    ).astype(F32)
    return (summed[None, :, :features], summed[None, :, features:])


def solution(mesh):
    placed = (
        P(None, "dp", None),
        P("section", None, None),
        P("section", None, None),
        P(),
        P(None, "dp"),
        P(None, "dp"),
        P(None, "dp"),
    )
    return jax.shard_map(
        shards,
        mesh=mesh,
        in_specs=placed,
        out_specs=(P("section", "dp", None), P("section", "dp", None)),
        check_vma=False,
    )
```

```python
import functools

import jax
import jax.numpy as jnp
from jax import lax
from jax.experimental import pallas as pl
from jax.experimental.pallas import tpu as pltpu
from jax.sharding import PartitionSpec as P

HD = 128
HEADS = 4
EPS = 1e-06
THETA = 1000000.0
SUB = 16
PIECES = 4
MESH = pl.DeviceIdType.MESH
F32 = jnp.float32
BF16 = jnp.bfloat16


def dot(left, right):
    return jnp.dot(left, right, preferred_element_type=F32)


def dot_t(left, right):
    return lax.dot_general(left, right, (((1,), (1,)), ((), ())), preferred_element_type=F32)


def t_dot(left, right):
    return lax.dot_general(left, right, (((0,), (0,)), ((), ())), preferred_element_type=F32)


def stack(array):
    return jnp.concatenate([array[:, h * HD : (h + 1) * HD] for h in range(HEADS)], axis=0)


def unstack(array):
    return jnp.concatenate([array[h * SUB : (h + 1) * SUB] for h in range(HEADS)], axis=1)


def swap(array):
    return pltpu.roll(array, HD // 2, 1)


def tall(array):
    return jnp.concatenate([array] * HEADS, axis=0)


def pipe_kernel(
    sections,
    x0,
    wk,
    wv,
    wscore,
    cosine,
    sine,
    mask,
    ends,
    target,
    out_key,
    out_value,
    hin,
    gin,
    gkv,
    mixs,
    hout,
    gout,
    keys,
    values,
    probs,
    scales,
    scores,
    oscales,
    gweights,
    carry_v,
    carry_k,
    peer_h,
    peer_g,
    peer_gkv,
    peer_mix,
    total,
    pair_out,
    pair_in,
    first_out,
    first_in,
    second_out,
    second_in,
    local_sem,
    hsend,
    hrecv,
    gsend,
    grecv,
    xsend,
    xrecv,
    pair_send,
    pair_recv,
    first_send,
    first_recv,
    second_send,
    second_recv,
):
    section = lax.axis_index("section")
    place = lax.axis_index("dp")
    x, y, core = place // 8, (place // 2) % 4, place % 2
    xpeers = [((x + r) % 4) * 8 + place % 8 for r in range(1, 4)]
    sibling = x * 8 + y * 2 + (1 - core)
    beside = y + 1 - 2 * (y % 2)
    across = 3 - y
    opposite = (y + 2) % 4
    ydevices = [x * 8 + beside * 2 + core, x * 8 + across * 2 + core]
    last = sections - 1
    chunks = hin.shape[0]
    model = hin.shape[2]
    piece = model // PIECES
    up = jnp.minimum(section + 1, last)
    down = jnp.maximum(section - 1, 0)

    barrier = pltpu.get_barrier_semaphore()

    @pl.when(section < last)
    def _():
        pl.semaphore_signal(barrier, inc=1, device_id={"section": up}, device_id_type=MESH)

    @pl.when(section > 0)
    def _():
        pl.semaphore_signal(barrier, inc=1, device_id={"section": down}, device_id_type=MESH)

    @pl.when(section == 0)
    def _():
        copy = pltpu.make_async_copy(x0, hin, local_sem)
        copy.start()
        copy.wait()

    keys[...] = jnp.zeros_like(keys)
    values[...] = jnp.zeros_like(values)

    for peer in xpeers + ydevices + [sibling]:
        pl.semaphore_signal(barrier, inc=1, device_id={"dp": peer}, device_id_type=MESH)

    @pl.when((section > 0) & (section < last))
    def _():
        pl.semaphore_wait(barrier, 8)

    @pl.when((section == 0) | (section == last))
    def _():
        pl.semaphore_wait(barrier, 7)

    def columns(p):
        return pl.ds(p * piece, piece)

    def h_copy(c, p):
        return pltpu.make_async_remote_copy(
            src_ref=hout.at[c, :, columns(p)],
            dst_ref=hin.at[c, :, columns(p)],
            send_sem=hsend.at[c, p],
            recv_sem=hrecv.at[c, p],
            device_id={"section": up},
            device_id_type=MESH,
        )

    def g_copy(c, p):
        return pltpu.make_async_remote_copy(
            src_ref=gout.at[c, :, columns(p)],
            dst_ref=gin.at[c, :, columns(p)],
            send_sem=gsend.at[c, p],
            recv_sem=grecv.at[c, p],
            device_id={"section": down},
            device_id_type=MESH,
        )

    def x_copy(kind, c, r):
        peer = (x + r) % 4
        source, target = (
            (hin.at[c, :, pl.ds(pl.multiple_of(peer * piece, 128), piece)], peer_h),
            (mixs.at[c], peer_mix),
            (gin.at[c, :, pl.ds(pl.multiple_of(peer * piece, 128), piece)], peer_g),
            (gkv.at[c], peer_gkv),
        )[kind]
        return pltpu.make_async_remote_copy(
            src_ref=source,
            dst_ref=target.at[r - 1, c],
            send_sem=xsend.at[kind, c, r - 1],
            recv_sem=xrecv.at[kind, c, r - 1],
            device_id={"dp": xpeers[r - 1]},
            device_id_type=MESH,
        )

    def forward(c):
        row = c // 2
        acc_k = jnp.zeros((SUB, HEADS * HD), F32)
        acc_v = jnp.zeros((SUB, HEADS * HD), F32)
        square = jnp.zeros((SUB, 1), F32)
        for p in range(PIECES):

            @pl.when(section > 0)
            def _():
                h_copy(c, p).wait_recv()

            part = hin[c, :, columns(p)]
            acc_k += dot(part, wk[columns(p), :])
            acc_v += dot(part, wv[columns(p), :])
            full = part.astype(F32)
            square += jnp.sum(full * full, axis=1, keepdims=True)
        scale = lax.rsqrt(square / model + EPS)
        scales[c] = scale
        turned = stack(acc_k * scale)
        turned = turned * tall(cosine[c]) + swap(turned) * tall(sine[c])
        key = turned.astype(BF16)
        value = stack(acc_v * scale).astype(BF16)
        keys[c] = key
        values[c] = value
        all_keys = keys[pl.ds(row * 2, 2)].reshape(2 * HEADS * SUB, HD)
        all_values = values[pl.ds(row * 2, 2)].reshape(2 * HEADS * SUB, HD)
        logits = dot_t(key, all_keys) * (1.0 / HD)
        logits = jnp.where(mask[c] > 0.0, logits, -1e30)
        top = jnp.max(logits, axis=1, keepdims=True)
        expd = jnp.exp(logits - top)
        prob = expd / jnp.sum(expd, axis=1, keepdims=True)
        probs[c] = prob
        mixed = unstack(dot(prob.astype(BF16), all_values).astype(BF16))
        mixs[c] = mixed
        for p in range(PIECES):
            out = hin[c, :, columns(p)].astype(F32) + dot_t(mixed, wv[columns(p), :])
            hout[c, :, columns(p)] = out.astype(BF16)

            @pl.when(section < last)
            def _():
                h_copy(c, p).start()

        for r in range(1, 4):
            x_copy(0, c, r).start()
            x_copy(1, c, r).start()

        @pl.when(section == last)
        def _():
            square = jnp.zeros((SUB, 1), F32)
            score = jnp.zeros((SUB, 1), F32)
            for p in range(PIECES):
                full = hout[c, :, columns(p)].astype(F32)
                square += jnp.sum(full * full, axis=1, keepdims=True)
                score += jnp.sum(full * wscore[:, columns(p)], axis=1, keepdims=True)
            scale = lax.rsqrt(square / model + EPS)
            oscales[c] = scale
            scores[c] = score * scale

    def backward(j):
        row = j // 2
        half = 1 - lax.rem(j, 2)
        c = row * 2 + half

        @pl.when(section == last)
        def _():
            both = pl.ds(row * 2, 2)
            end = ends[both]
            score = scores[both]
            masked = jnp.where(end > 0.0, score, -1e30)
            top = jnp.max(jnp.max(masked, axis=0), axis=0, keepdims=True)
            expd = jnp.where(end > 0.0, jnp.exp(masked - top[None]), 0.0)
            total = jnp.sum(jnp.sum(expd, axis=0), axis=0, keepdims=True)
            gweights[...] = jnp.where(end > 0.0, expd / total[None] - target[both], 0.0)
            weight = gweights[half]
            scale = oscales[c]
            first = scale * weight
            second = scale * scale * weight * scores[c] * (1.0 / model)
            for p in range(PIECES):
                full = hout[c, :, columns(p)].astype(F32)
                gin[c, :, columns(p)] = (first * wscore[:, columns(p)] - second * full).astype(BF16)

        acc = jnp.zeros((SUB, HEADS * HD), F32)
        for p in range(PIECES):

            @pl.when(section < last)
            def _():
                g_copy(c, p).wait_recv()

            acc += dot(gin[c, :, columns(p)], wv[columns(p), :])
        scale = scales[c]
        grad_mixed = stack(acc).astype(BF16)
        all_keys = keys[pl.ds(row * 2, 2)].reshape(2 * HEADS * SUB, HD)
        all_values = values[pl.ds(row * 2, 2)].reshape(2 * HEADS * SUB, HD)
        key = keys[c]
        value = values[c]
        prob = probs[c]
        grad_probs = dot_t(grad_mixed, all_values)
        product = prob * grad_probs
        grad_scores = (product - prob * jnp.sum(product, axis=1, keepdims=True)).astype(BF16)
        from_v = t_dot(prob.astype(BF16), grad_mixed)
        from_k = t_dot(grad_scores, key)
        lower = HEADS * SUB
        second = half == 1
        own_v = jnp.where(second, from_v[lower:], from_v[:lower] + carry_v[...])
        own_k = jnp.where(second, from_k[lower:], from_k[:lower] + carry_k[...])
        carry_v[...] = from_v[:lower]
        carry_k[...] = from_k[:lower]
        turned = (dot(grad_scores, all_keys) + own_k) * (1.0 / HD)
        grad_value = own_v.astype(BF16)
        along = jnp.sum(turned * key.astype(F32) + own_v * value.astype(F32), axis=1, keepdims=True)
        along = along[:SUB] + along[SUB : 2 * SUB] + along[2 * SUB : 3 * SUB] + along[3 * SUB :]
        along = along * (scale * scale) * (1.0 / model)
        grad_key = (turned * tall(cosine[c]) - swap(turned) * tall(sine[c])).astype(BF16)
        flat_key = unstack(grad_key)
        flat_value = unstack(grad_value)
        features = HEADS * HD
        gkv[c, :, :features] = (flat_key.astype(F32) * scale).astype(BF16)
        gkv[c, :, features:] = (flat_value.astype(F32) * scale).astype(BF16)

        @pl.when(section > 0)
        def _():
            for p in range(PIECES):
                grad = dot_t(flat_key, wk[columns(p), :]) + dot_t(flat_value, wv[columns(p), :])
                out = (
                    gin[c, :, columns(p)].astype(F32)
                    + scale * grad
                    - along * hin[c, :, columns(p)].astype(F32)
                )
                gout[c, :, columns(p)] = out.astype(BF16)
                g_copy(c, p).start()

        for r in range(1, 4):
            x_copy(2, c, r).start()
            x_copy(3, c, r).start()

    tile = 256
    group = chunks // 2

    def weights(base, again):
        def arrive(c, unused):
            for kind in range(4):
                for r in range(1, 4):
                    x_copy(kind, base + c, r).wait_recv()
            return unused

        lax.fori_loop(0, group, arrive, 0)
        which = pl.ds(base, group)

        def gather(own, peers):
            own = own.reshape(group * SUB, own.shape[-1])
            peers = peers.reshape(3 * group * SUB, peers.shape[-1])
            return jnp.concatenate([own, peers], axis=0)

        def block(t, unused):
            there = pl.ds(pl.multiple_of(t * tile, tile), tile)
            mine = pl.ds(pl.multiple_of(x * piece + t * tile, 128), tile)
            hidden = gather(hin[which, :, mine], peer_h[:, which, :, there])
            grads = gather(gin[which, :, mine], peer_g[:, which, :, there])
            both = gather(gkv[which], peer_gkv[:, which])
            mixed = gather(mixs[which], peer_mix[:, which])
            features = HEADS * HD
            part_key = t_dot(hidden, both[:, :features])
            part_value = t_dot(hidden, both[:, features:]) + t_dot(grads, mixed)
            if again:
                part_key = part_key + total[there, :features]
                part_value = part_value + total[there, features:]
            total[there, :features] = part_key
            total[there, features:] = part_value
            return unused

        lax.fori_loop(0, piece // tile, block, 0)

    share = piece // 8
    half_features = HEADS * HD
    sides = [pl.ds(0, half_features), pl.ds(half_features, half_features)]

    def rows_of(ypart, corepart):
        return pl.ds(pl.multiple_of((ypart * 2 + corepart) * share, 32), share)

    def pair_copy(k):
        return pltpu.make_async_remote_copy(
            src_ref=pair_out.at[k],
            dst_ref=pair_in.at[k],
            send_sem=pair_send.at[k],
            recv_sem=pair_recv.at[k],
            device_id={"dp": sibling},
            device_id_type=MESH,
        )

    def first_copy(side, k):
        return pltpu.make_async_remote_copy(
            src_ref=first_out.at[side, k],
            dst_ref=first_in.at[side, k],
            send_sem=first_send.at[side, k],
            recv_sem=first_recv.at[side, k],
            device_id={"dp": ydevices[side]},
            device_id_type=MESH,
        )

    def second_copy(side):
        return pltpu.make_async_remote_copy(
            src_ref=second_out.at[side],
            dst_ref=second_in.at[side],
            send_sem=second_send.at[side],
            recv_sem=second_recv.at[side],
            device_id={"dp": ydevices[1 - side]},
            device_id_type=MESH,
        )

    def scatter():
        order = [opposite, beside, across, y]
        for k in range(4):
            pair_out[k] = total[rows_of(order[k], 1 - core), :].astype(BF16)
            pair_copy(k).start()

        def held(k, side):
            return total[rows_of(order[k], core), sides[side]] + pair_in[k, :, sides[side]].astype(F32)

        pair_copy(0).wait_recv()
        for side in range(2):
            first_out[side, 1] = held(0, side).astype(BF16)
            first_copy(side, 1).start()
        for side in range(2):
            pair_copy(1 + side).wait_recv()
            first_out[side, 0] = held(1 + side, side).astype(BF16)
            first_copy(side, 0).start()
        for side in range(2):
            first_copy(side, 1).wait_recv()
            second_out[side] = (held(2 - side, side) + first_in[side, 1].astype(F32)).astype(BF16)
            second_copy(side).start()
        pair_copy(3).wait_recv()
        for side, out in ((0, out_key), (1, out_value)):
            first_copy(side, 0).wait_recv()
            second_copy(side).wait_recv()
            out[...] = held(3, side) + first_in[side, 0].astype(F32) + second_in[side].astype(F32)
        for k in range(4):
            pair_copy(k).wait_send()
        for side in range(2):
            first_copy(side, 0).wait_send()
            first_copy(side, 1).wait_send()
            second_copy(side).wait_send()

    lead = jnp.where(section == last, 1, jnp.where(section == last - 1, 5, chunks))

    def slot(i, unused):
        @pl.when(i < chunks)
        def _():
            forward(i)

        j = i - lead

        @pl.when((j >= 0) & (j < chunks))
        def _():
            backward(j)

        @pl.when(j == group + 1)
        def _():
            weights(0, False)

        return unused

    lax.fori_loop(0, 2 * chunks, slot, 0)
    weights(group, True)
    scatter()

    def drain(c, unused):
        for p in range(PIECES):

            @pl.when(section < last)
            def _():
                h_copy(c, p).wait_send()

            @pl.when(section > 0)
            def _():
                g_copy(c, p).wait_send()

        for kind in range(4):
            for r in range(1, 4):
                x_copy(kind, c, r).wait_send()
        return unused

    lax.fori_loop(0, chunks, drain, 0)


def tables(segments, lengths, grades):
    micro, width = segments.shape
    index = jnp.arange(width, dtype=jnp.int32)
    change = segments[:, 1:] != segments[:, :-1]
    starts = jnp.concatenate([jnp.ones((micro, 1), bool), change], axis=1)
    same = segments[:, :, None] == segments[:, None, :]
    first = jnp.max(jnp.where(starts[:, None, :] & (index[None, :] <= index[:, None]), index, 0), axis=2)
    offset = (index - first).astype(F32)
    freqs = THETA ** (-(jnp.arange(HD // 2, dtype=F32) * 2.0) / HD)
    angles = offset[..., None] * freqs
    cosine, sine = jnp.cos(angles), jnp.sin(angles)
    chunks = micro * width // SUB
    cosine = jnp.concatenate([cosine, cosine], axis=-1).reshape(chunks, SUB, HD)
    sine = jnp.concatenate([-sine, sine], axis=-1).reshape(chunks, SUB, HD)
    live = index < lengths
    causal = index[None, :] <= index[:, None]
    allowed = same & causal & live[:, :, None] & live[:, None, :]
    allowed = allowed | jnp.eye(width, dtype=bool)
    halves = width // SUB
    allowed = allowed.reshape(micro, halves, 1, SUB, halves, 1, SUB)
    heads = jnp.eye(HEADS, dtype=bool).reshape(1, 1, HEADS, 1, 1, HEADS, 1)
    mask = (allowed & heads).astype(F32).reshape(chunks, HEADS * SUB, halves * HEADS * SUB)
    following = jnp.concatenate([change, jnp.ones((micro, 1), bool)], axis=1)
    ends = live & (following | (index == lengths - 1))
    target = jax.nn.softmax(jnp.where(ends, grades.astype(F32), -1e30), axis=-1)
    ends = ends.astype(F32).reshape(chunks, SUB, 1)
    target = target.reshape(chunks, SUB, 1)
    return cosine, sine, mask, ends, target


def shards(x0, w_key, w_value, w_score, segments, lengths, grades):
    sections = lax.axis_size("section")
    micro, width, model = x0.shape
    features = w_key.shape[2]
    chunks = micro * width // SUB
    cosine, sine, mask, ends, target = tables(segments, lengths, grades)
    vmem = pl.BlockSpec(memory_space=pltpu.VMEM)
    act = (chunks, SUB, model)
    flat = (chunks, SUB, features)
    stacked = (chunks, HEADS * SUB, HD)
    piece = model // PIECES
    share = piece // 8
    dma = pltpu.SemaphoreType.DMA
    grad_key, grad_value = pl.pallas_call(
        functools.partial(pipe_kernel, sections),
        out_shape=[jax.ShapeDtypeStruct((share, features), F32)] * 2,
        in_specs=[pl.BlockSpec(memory_space=pl.ANY)] + [vmem] * 8,
        out_specs=[vmem] * 2,
        scratch_shapes=[
            pltpu.VMEM(act, BF16),
            pltpu.VMEM(act, BF16),
            pltpu.VMEM((chunks, SUB, 2 * features), BF16),
            pltpu.VMEM(flat, BF16),
            pltpu.VMEM(act, BF16),
            pltpu.VMEM(act, BF16),
            pltpu.VMEM(stacked, BF16),
            pltpu.VMEM(stacked, BF16),
            pltpu.VMEM((chunks, HEADS * SUB, 2 * HEADS * SUB), F32),
            pltpu.VMEM((chunks, SUB, 1), F32),
            pltpu.VMEM((chunks, SUB, 1), F32),
            pltpu.VMEM((chunks, SUB, 1), F32),
            pltpu.VMEM((2, SUB, 1), F32),
            pltpu.VMEM((HEADS * SUB, HD), F32),
            pltpu.VMEM((HEADS * SUB, HD), F32),
            pltpu.VMEM((3, chunks, SUB, piece), BF16),
            pltpu.VMEM((3, chunks, SUB, piece), BF16),
            pltpu.VMEM((3, chunks, SUB, 2 * features), BF16),
            pltpu.VMEM((3, chunks, SUB, features), BF16),
            pltpu.VMEM((piece, 2 * features), F32),
            pltpu.VMEM((4, share, 2 * features), BF16),
            pltpu.VMEM((4, share, 2 * features), BF16),
            pltpu.VMEM((2, 2, share, features), BF16),
            pltpu.VMEM((2, 2, share, features), BF16),
            pltpu.VMEM((2, share, features), BF16),
            pltpu.VMEM((2, share, features), BF16),
            dma,
            dma((chunks, PIECES)),
            dma((chunks, PIECES)),
            dma((chunks, PIECES)),
            dma((chunks, PIECES)),
            dma((4, chunks, 3)),
            dma((4, chunks, 3)),
            dma((4,)),
            dma((4,)),
            dma((2, 2)),
            dma((2, 2)),
            dma((2,)),
            dma((2,)),
        ],
        compiler_params=pltpu.CompilerParams(
            collective_id=0, has_side_effects=True, vmem_limit_bytes=56 * 2**20
        ),
    )(
        x0.reshape(act),
        w_key[0],
        w_value[0],
        w_score.reshape(1, model),
        cosine,
        sine,
        mask,
        ends,
        target,
    )
    return (grad_key[None], grad_value[None])


def solution(mesh):
    placed = (
        P(None, "dp", None),
        P("section", None, None),
        P("section", None, None),
        P(),
        P(None, "dp"),
        P(None, "dp"),
        P(None, "dp"),
    )
    return jax.shard_map(
        shards,
        mesh=mesh,
        in_specs=placed,
        out_specs=(P("section", "dp", None), P("section", "dp", None)),
        check_vma=False,
    )
```

```python
import functools
import math

import jax
import jax.numpy as jnp
from jax import lax
from jax.experimental import pallas as pl
from jax.experimental.pallas import tpu as pltpu
from jax.sharding import PartitionSpec as P

HD = 128
HEADS = 4
EPS = 1e-06
THETA = 1000000.0
SUB = 16
PIECES = 4
MESH = pl.DeviceIdType.MESH
F32 = jnp.float32
BF16 = jnp.bfloat16


def dot(left, right):
    return jnp.dot(left, right, preferred_element_type=F32)


def dot_t(left, right):
    return lax.dot_general(left, right, (((1,), (1,)), ((), ())), preferred_element_type=F32)


def t_dot(left, right):
    return lax.dot_general(left, right, (((0,), (0,)), ((), ())), preferred_element_type=F32)


def stack(array):
    blocks = []
    for start in range(0, array.shape[0], SUB):
        blocks += [array[start : start + SUB, h * HD : (h + 1) * HD] for h in range(HEADS)]
    return jnp.concatenate(blocks, axis=0)


def unstack(array):
    rows = []
    for start in range(0, array.shape[0], HEADS * SUB):
        blocks = [array[start + h * SUB : start + (h + 1) * SUB] for h in range(HEADS)]
        rows.append(jnp.concatenate(blocks, axis=1))
    return jnp.concatenate(rows, axis=0)


def swap(array):
    return pltpu.roll(array, HD // 2, 1)


def tall(array):
    return jnp.concatenate([array[k] for k in range(array.shape[0]) for h in range(HEADS)], axis=0)


def pipe_kernel(
    sections,
    x0,
    wk_all,
    wv_all,
    wscore,
    segments,
    lengths,
    grades,
    out_key,
    out_value,
    wk,
    wv,
    wkt,
    wvt,
    slots,
    cosine,
    sine,
    mask,
    ends,
    levels,
    hin,
    gin,
    gkv,
    mixs,
    hout,
    gout,
    keys,
    values,
    probs,
    scales,
    carry_v,
    carry_k,
    peer_h,
    peer_g,
    peer_gkv,
    peer_mix,
    total,
    pair_out,
    pair_in,
    first_out,
    first_in,
    second_out,
    second_in,
    local_sem,
    weight_sem,
    hsend,
    hrecv,
    gsend,
    grecv,
    xsend,
    xrecv,
    pair_send,
    pair_recv,
    first_send,
    first_recv,
    second_send,
    second_recv,
):
    section = lax.axis_index("section")
    place = lax.axis_index("dp")
    x, y, core = place // 8, (place // 2) % 4, place % 2
    xpeers = [((x + r) % 4) * 8 + place % 8 for r in range(1, 4)]
    sibling = x * 8 + y * 2 + (1 - core)
    beside = y + 1 - 2 * (y % 2)
    across = 3 - y
    opposite = (y + 2) % 4
    ydevices = [x * 8 + beside * 2 + core, x * 8 + across * 2 + core]
    last = sections - 1
    chunks = hin.shape[0]
    model = hin.shape[2]
    piece = model // PIECES
    up = jnp.minimum(section + 1, last)
    down = jnp.maximum(section - 1, 0)

    rows = HEADS * SUB
    load_k = pltpu.make_async_copy(wk_all, wk, weight_sem.at[0])
    load_v = pltpu.make_async_copy(wv_all, wv, weight_sem.at[1])
    load_x = pltpu.make_async_copy(x0, hin, local_sem)
    load_k.start()
    load_v.start()

    @pl.when(section == 0)
    def _():
        load_x.start()

    barrier = pltpu.get_barrier_semaphore()

    @pl.when(section < last)
    def _():
        pl.semaphore_signal(barrier, inc=1, device_id={"section": up}, device_id_type=MESH)

    @pl.when(section > 0)
    def _():
        pl.semaphore_signal(barrier, inc=1, device_id={"section": down}, device_id_type=MESH)

    for peer in xpeers + ydevices + [sibling]:
        pl.semaphore_signal(barrier, inc=1, device_id={"dp": peer}, device_id_type=MESH)

    keys[...] = jnp.zeros_like(keys)
    values[...] = jnp.zeros_like(values)
    source = lax.broadcasted_iota(jnp.int32, (slots.shape[0] * 4, 2 * rows), 0)
    lane = lax.broadcasted_iota(jnp.int32, (slots.shape[0] * 4, 2 * rows), 1)
    spread = (source == (lane // rows) * SUB + lane % SUB).astype(BF16)
    both = jnp.concatenate([segments[...], grades[...]], axis=0).astype(F32).astype(BF16)
    slots[...] = dot(both, spread)

    def make_tables(c, unused):
        row, half = c // 2, lax.rem(c, 2)
        sub = lax.broadcasted_iota(jnp.int32, (rows, 2 * rows), 0)
        lane = lax.broadcasted_iota(jnp.int32, (rows, 2 * rows), 1)
        slot_i = half * SUB + sub % SUB
        slot_j = (lane // rows) * SUB + lane % SUB
        seg_j = jnp.broadcast_to(slots[pl.ds(row, 1), :], (rows, 2 * rows))
        grade_j = jnp.broadcast_to(slots[pl.ds(row + chunks // 2, 1), :], (rows, 2 * rows))
        here = lane == half * rows + sub
        seg_i = jnp.sum(jnp.where(here, seg_j, 0.0), axis=1, keepdims=True)
        grade_i = jnp.sum(jnp.where(here, grade_j, 0.0), axis=1, keepdims=True)
        length = jnp.broadcast_to(lengths[pl.ds(row, 1), :], (rows, 2 * rows))
        same = seg_j == seg_i
        live = slot_i < length
        allowed = (same & (slot_j <= slot_i) & live & (slot_j < length)) | (slot_i == slot_j)
        heads = sub // SUB == (lane // SUB) % HEADS
        mask[c] = jnp.where(allowed & heads, 1.0, 0.0)
        once = (lane // SUB) % HEADS == 0
        before = jnp.sum(jnp.where(once & (seg_j < seg_i), 1.0, 0.0), axis=1, keepdims=True)
        after = jnp.sum(
            jnp.where(once & same & (slot_j > slot_i), 1.0, 0.0), axis=1, keepdims=True
        )
        final = (after == 0.0) | (slot_i == length - 1)
        ends[c] = jnp.where(live & final, 1.0, 0.0)[:SUB, :1]
        levels[c] = grade_i[:SUB]
        position = slot_i[:SUB].astype(F32) - before[:SUB]
        lane = lane[:SUB]
        freqs = jnp.exp((lane % (HD // 2)).astype(F32) * (-2.0 * math.log(THETA) / HD))
        angles = position * freqs
        cosine[c] = jnp.cos(angles)
        sine[c] = jnp.where(lane < HD // 2, -1.0, 1.0) * jnp.sin(angles)
        return unused

    lax.fori_loop(0, chunks, make_tables, 0)

    @pl.when(section == 0)
    def _():
        load_x.wait()

    load_k.wait()
    load_v.wait()

    @pl.when((section > 0) & (section < last))
    def _():
        pl.semaphore_wait(barrier, 8)

    @pl.when((section == 0) | (section == last))
    def _():
        pl.semaphore_wait(barrier, 7)

    def turn(source, target):
        def block(t, unused):
            there = pl.ds(pl.multiple_of(t * 256, 256), 256)
            target[:, there] = source[there, :].T
            return unused

        lax.fori_loop(0, model // 256, block, 0)

    @pl.when(section > 0)
    def _():
        turn(wv, wvt)

    @pl.when(section > 1)
    def _():
        turn(wk, wkt)

    def columns(p):
        return pl.ds(p * piece, piece)

    def h_copy(c, p):
        return pltpu.make_async_remote_copy(
            src_ref=hout.at[c, :, columns(p)],
            dst_ref=hin.at[c, :, columns(p)],
            send_sem=hsend.at[c, p],
            recv_sem=hrecv.at[c, p],
            device_id={"section": up},
            device_id_type=MESH,
        )

    def g_copy(c, p):
        return pltpu.make_async_remote_copy(
            src_ref=gout.at[c, :, columns(p)],
            dst_ref=gin.at[c, :, columns(p)],
            send_sem=gsend.at[c, p],
            recv_sem=grecv.at[c, p],
            device_id={"section": down},
            device_id_type=MESH,
        )

    def x_copy(kind, c, r):
        peer = (x + r) % 4
        source, target = (
            (hin.at[c, :, pl.ds(pl.multiple_of(peer * piece, 128), piece)], peer_h),
            (mixs.at[c], peer_mix),
            (gin.at[c, :, pl.ds(pl.multiple_of(peer * piece, 128), piece)], peer_g),
            (gkv.at[c], peer_gkv),
        )[kind]
        return pltpu.make_async_remote_copy(
            src_ref=source,
            dst_ref=target.at[r - 1, c],
            send_sem=xsend.at[kind, c, r - 1],
            recv_sem=xrecv.at[kind, c, r - 1],
            device_id={"dp": xpeers[r - 1]},
            device_id_type=MESH,
        )

    def forward(c, n):
        some = pl.ds(c, n)
        lines = n * SUB
        row = c // 2

        def held(p):
            return hin[some, :, columns(p)].reshape(lines, piece)

        acc_k = jnp.zeros((lines, HEADS * HD), F32)
        acc_v = jnp.zeros((lines, HEADS * HD), F32)
        square = jnp.zeros((lines, 1), F32)
        for p in range(PIECES):

            @pl.when(section > 0)
            def _():
                for k in range(n):
                    h_copy(c + k, p).wait_recv()

            part = held(p)
            acc_k += dot(part, wk[columns(p), :])
            acc_v += dot(part, wv[columns(p), :])
            full = part.astype(F32)
            square += jnp.sum(full * full, axis=1, keepdims=True)
        scale = lax.rsqrt(square / model + EPS)
        scales[some] = scale.reshape(n, SUB, 1)
        turned = stack(acc_k * scale)
        turned = turned * tall(cosine[some]) + swap(turned) * tall(sine[some])
        key = turned.astype(BF16)
        value = stack(acc_v * scale).astype(BF16)
        keys[some] = key.reshape(n, rows, HD)
        values[some] = value.reshape(n, rows, HD)
        all_keys = keys[pl.ds(row * 2, 2)].reshape(2 * rows, HD)
        all_values = values[pl.ds(row * 2, 2)].reshape(2 * rows, HD)
        logits = dot_t(key, all_keys) * (1.0 / HD)
        logits = jnp.where(mask[some].reshape(n * rows, 2 * rows) > 0.0, logits, -1e30)
        top = jnp.max(logits, axis=1, keepdims=True)
        expd = jnp.exp(logits - top)
        prob = expd / jnp.sum(expd, axis=1, keepdims=True)
        probs[some] = prob.reshape(n, rows, 2 * rows)
        mixed = unstack(dot(prob.astype(BF16), all_values).astype(BF16))
        mixs[some] = mixed.reshape(n, SUB, HEADS * HD)

        def output(p, product):
            out = held(p).astype(F32) + product
            hout[some, :, columns(p)] = out.astype(BF16).reshape(n, SUB, piece)

        if n == 1:

            @pl.when(section == 0)
            def _():
                for p in range(PIECES):
                    output(p, dot_t(mixed, wv[columns(p), :]))
                    h_copy(c, p).start()

            @pl.when(section > 0)
            def _():
                for p in range(PIECES):
                    output(p, dot(mixed, wvt[:, columns(p)]))
                    h_copy(c, p).start()

        else:
            for p in range(PIECES):
                output(p, dot(mixed, wvt[:, columns(p)]))

        for k in range(n):
            for r in range(1, 4):
                x_copy(0, c + k, r).start()
                x_copy(1, c + k, r).start()

    def loss(c):
        some = pl.ds(c, 2)
        square = jnp.zeros((2, SUB, 1), F32)
        score = jnp.zeros((2, SUB, 1), F32)
        for p in range(PIECES):
            full = hout[some, :, columns(p)].astype(F32)
            square += jnp.sum(full * full, axis=2, keepdims=True)
            score += jnp.sum(full * wscore[:, columns(p)][None], axis=2, keepdims=True)
        scale = lax.rsqrt(square / model + EPS)
        score = score * scale
        end = ends[some]

        def softmax(entries):
            masked = jnp.where(end > 0.0, entries, -1e30)
            top = jnp.max(jnp.max(masked, axis=0), axis=0, keepdims=True)
            expd = jnp.where(end > 0.0, jnp.exp(masked - top[None]), 0.0)
            return expd / jnp.sum(jnp.sum(expd, axis=0), axis=0, keepdims=True)[None]

        weight = jnp.where(end > 0.0, softmax(score) - softmax(levels[some]), 0.0)
        first = scale * weight
        second = scale * scale * weight * score * (1.0 / model)
        for p in range(PIECES):
            full = hout[some, :, columns(p)].astype(F32)
            grad = first * wscore[:, columns(p)][None] - second * full
            gin[some, :, columns(p)] = grad.astype(BF16)

    def backward(c, n):
        some = pl.ds(c, n)
        lines = n * SUB
        row = c // 2

        def grad_at(p):
            return gin[some, :, columns(p)].reshape(lines, piece)

        acc = jnp.zeros((lines, HEADS * HD), F32)
        for p in range(PIECES):
            if n == 1:
                g_copy(c, p).wait_recv()
            acc += dot(grad_at(p), wv[columns(p), :])
        scale = scales[some].reshape(lines, 1)
        grad_mixed = stack(acc).astype(BF16)
        all_keys = keys[pl.ds(row * 2, 2)].reshape(2 * rows, HD)
        all_values = values[pl.ds(row * 2, 2)].reshape(2 * rows, HD)
        key = keys[some].reshape(n * rows, HD)
        value = values[some].reshape(n * rows, HD)
        prob = probs[some].reshape(n * rows, 2 * rows)
        grad_probs = dot_t(grad_mixed, all_values)
        product = prob * grad_probs
        grad_scores = (product - prob * jnp.sum(product, axis=1, keepdims=True)).astype(BF16)
        own_v = t_dot(prob.astype(BF16), grad_mixed)
        own_k = t_dot(grad_scores, key)
        if n == 1:
            second = lax.rem(c, 2) == 1
            from_v, from_k = own_v, own_k
            own_v = jnp.where(second, from_v[rows:], from_v[:rows] + carry_v[...])
            own_k = jnp.where(second, from_k[rows:], from_k[:rows] + carry_k[...])
            carry_v[...] = from_v[:rows]
            carry_k[...] = from_k[:rows]
        turned = (dot(grad_scores, all_keys) + own_k) * (1.0 / HD)
        along = jnp.sum(turned * key.astype(F32) + own_v * value.astype(F32), axis=1, keepdims=True)
        along = jnp.sum(along.reshape(n, HEADS, SUB, 1), axis=1).reshape(lines, 1)
        along = along * (scale * scale) * (1.0 / model)
        grad_key = turned * tall(cosine[some]) - swap(turned) * tall(sine[some])
        flat_key = unstack(grad_key.astype(BF16))
        flat_value = unstack(own_v.astype(BF16))
        features = HEADS * HD
        key_part = (flat_key.astype(F32) * scale).astype(BF16)
        value_part = (flat_value.astype(F32) * scale).astype(BF16)
        gkv[some, :, :features] = key_part.reshape(n, SUB, features)
        gkv[some, :, features:] = value_part.reshape(n, SUB, features)

        @pl.when(section > 0)
        def _():
            for p in range(PIECES):
                grad = dot(flat_key, wkt[:, columns(p)]) + dot(flat_value, wvt[:, columns(p)])
                full = hin[some, :, columns(p)].reshape(lines, piece).astype(F32)
                out = grad_at(p).astype(F32) + scale * grad - along * full
                gout[some, :, columns(p)] = out.astype(BF16).reshape(n, SUB, piece)
                g_copy(c + n - 1, p).start()
            if n == 2:
                for p in range(PIECES):
                    g_copy(c, p).start()

        for k in range(n):
            for r in range(1, 4):
                x_copy(2, c + k, r).start()
                x_copy(3, c + k, r).start()

    tile = 256
    group = chunks // 2

    def weights(base):
        def arrive(c, unused):
            for kind in range(4):
                for r in range(1, 4):
                    x_copy(kind, base + c, r).wait_recv()
            return unused

        lax.fori_loop(0, group, arrive, 0)
        which = pl.ds(base, group)

        def gather(own, peers):
            own = own.reshape(group * SUB, own.shape[-1])
            peers = peers.reshape(3 * group * SUB, peers.shape[-1])
            return jnp.concatenate([own, peers], axis=0)

        def block(t, unused):
            there = pl.ds(pl.multiple_of(t * tile, tile), tile)
            mine = pl.ds(pl.multiple_of(x * piece + t * tile, 128), tile)
            hidden = gather(hin[which, :, mine], peer_h[:, which, :, there])
            grads = gather(gin[which, :, mine], peer_g[:, which, :, there])
            both = gather(gkv[which], peer_gkv[:, which])
            mixed = gather(mixs[which], peer_mix[:, which])
            features = HEADS * HD
            part_key = t_dot(hidden, both[:, :features])
            part_value = t_dot(hidden, both[:, features:]) + t_dot(grads, mixed)

            @pl.when(base == 0)
            def _():
                total[there, :features] = part_key
                total[there, features:] = part_value

            @pl.when(base > 0)
            def _():
                total[there, :features] = part_key + total[there, :features]
                total[there, features:] = part_value + total[there, features:]

            return unused

        lax.fori_loop(0, piece // tile, block, 0)

    share = piece // 8
    half_features = HEADS * HD
    sides = [pl.ds(0, half_features), pl.ds(half_features, half_features)]

    def rows_of(ypart, corepart):
        return pl.ds(pl.multiple_of((ypart * 2 + corepart) * share, 32), share)

    def pair_copy(k):
        return pltpu.make_async_remote_copy(
            src_ref=pair_out.at[k],
            dst_ref=pair_in.at[k],
            send_sem=pair_send.at[k],
            recv_sem=pair_recv.at[k],
            device_id={"dp": sibling},
            device_id_type=MESH,
        )

    def first_copy(side, k):
        return pltpu.make_async_remote_copy(
            src_ref=first_out.at[side, k],
            dst_ref=first_in.at[side, k],
            send_sem=first_send.at[side, k],
            recv_sem=first_recv.at[side, k],
            device_id={"dp": ydevices[side]},
            device_id_type=MESH,
        )

    def second_copy(side):
        return pltpu.make_async_remote_copy(
            src_ref=second_out.at[side],
            dst_ref=second_in.at[side],
            send_sem=second_send.at[side],
            recv_sem=second_recv.at[side],
            device_id={"dp": ydevices[1 - side]},
            device_id_type=MESH,
        )

    def scatter():
        order = [opposite, beside, across, y]
        for k in range(4):
            pair_out[k] = total[rows_of(order[k], 1 - core), :].astype(BF16)
            pair_copy(k).start()

        def held(k, side):
            return total[rows_of(order[k], core), sides[side]] + pair_in[k, :, sides[side]].astype(F32)

        pair_copy(0).wait_recv()
        for side in range(2):
            first_out[side, 1] = held(0, side).astype(BF16)
            first_copy(side, 1).start()
        for side in range(2):
            pair_copy(1 + side).wait_recv()
            first_out[side, 0] = held(1 + side, side).astype(BF16)
            first_copy(side, 0).start()
        for side in range(2):
            first_copy(side, 1).wait_recv()
            second_out[side] = (held(2 - side, side) + first_in[side, 1].astype(F32)).astype(BF16)
            second_copy(side).start()
        pair_copy(3).wait_recv()
        for side, out in ((0, out_key), (1, out_value)):
            first_copy(side, 0).wait_recv()
            second_copy(side).wait_recv()
            out[...] = held(3, side) + first_in[side, 0].astype(F32) + second_in[side].astype(F32)
        for k in range(4):
            pair_copy(k).wait_send()
        for side in range(2):
            first_copy(side, 0).wait_send()
            first_copy(side, 1).wait_send()
            second_copy(side).wait_send()

    lead = jnp.where(section == last - 1, 5, chunks)

    def slot(i, unused):
        @pl.when(i < chunks)
        def _():
            forward(i, 1)

        j = i - lead

        @pl.when((j == 0) & (section == 1))
        def _():
            turn(wk, wkt)

        @pl.when((j >= 0) & (j < chunks))
        def _():
            backward((j // 2) * 2 + 1 - lax.rem(j, 2), 1)

        @pl.when(j == group + 1)
        def _():
            weights(0)

        return unused

    def whole(row, unused):
        forward(row * 2, 2)
        loss(row * 2)
        backward(row * 2, 2)
        return unused

    @pl.when(section < last)
    def _():
        lax.fori_loop(0, 2 * chunks, slot, 0)

    @pl.when(section == last)
    def _():
        lax.fori_loop(0, chunks // 2, whole, 0)

    def rest(step, unused):
        weights(step * group)
        return unused

    lax.fori_loop(jnp.where(section == last, 0, 1), 2, rest, 0)
    scatter()

    def drain(c, unused):
        for p in range(PIECES):

            @pl.when(section < last)
            def _():
                h_copy(c, p).wait_send()

            @pl.when(section > 0)
            def _():
                g_copy(c, p).wait_send()

        for kind in range(4):
            for r in range(1, 4):
                x_copy(kind, c, r).wait_send()
        return unused

    lax.fori_loop(0, chunks, drain, 0)


def shards(x0, w_key, w_value, w_score, segments, lengths, grades):
    sections = lax.axis_size("section")
    micro, width, model = x0.shape
    features = w_key.shape[2]
    chunks = micro * width // SUB
    vmem = pl.BlockSpec(memory_space=pltpu.VMEM)
    act = (chunks, SUB, model)
    flat = (chunks, SUB, features)
    stacked = (chunks, HEADS * SUB, HD)
    piece = model // PIECES
    share = piece // 8
    dma = pltpu.SemaphoreType.DMA
    grad_key, grad_value = pl.pallas_call(
        functools.partial(pipe_kernel, sections),
        out_shape=[jax.ShapeDtypeStruct((share, features), F32)] * 2,
        in_specs=[pl.BlockSpec(memory_space=pl.ANY)] * 3 + [vmem] * 4,
        out_specs=[vmem] * 2,
        scratch_shapes=[
            pltpu.VMEM((model, features), BF16),
            pltpu.VMEM((model, features), BF16),
            pltpu.VMEM((features, model), BF16),
            pltpu.VMEM((features, model), BF16),
            pltpu.VMEM((2 * micro, HD), F32),
            pltpu.VMEM((chunks, SUB, HD), F32),
            pltpu.VMEM((chunks, SUB, HD), F32),
            pltpu.VMEM((chunks, HEADS * SUB, 2 * HEADS * SUB), F32),
            pltpu.VMEM((chunks, SUB, 1), F32),
            pltpu.VMEM((chunks, SUB, 1), F32),
            pltpu.VMEM(act, BF16),
            pltpu.VMEM(act, BF16),
            pltpu.VMEM((chunks, SUB, 2 * features), BF16),
            pltpu.VMEM(flat, BF16),
            pltpu.VMEM(act, BF16),
            pltpu.VMEM(act, BF16),
            pltpu.VMEM(stacked, BF16),
            pltpu.VMEM(stacked, BF16),
            pltpu.VMEM((chunks, HEADS * SUB, 2 * HEADS * SUB), F32),
            pltpu.VMEM((chunks, SUB, 1), F32),
            pltpu.VMEM((HEADS * SUB, HD), F32),
            pltpu.VMEM((HEADS * SUB, HD), F32),
            pltpu.VMEM((3, chunks, SUB, piece), BF16),
            pltpu.VMEM((3, chunks, SUB, piece), BF16),
            pltpu.VMEM((3, chunks, SUB, 2 * features), BF16),
            pltpu.VMEM((3, chunks, SUB, features), BF16),
            pltpu.VMEM((piece, 2 * features), F32),
            pltpu.VMEM((4, share, 2 * features), BF16),
            pltpu.VMEM((4, share, 2 * features), BF16),
            pltpu.VMEM((2, 2, share, features), BF16),
            pltpu.VMEM((2, 2, share, features), BF16),
            pltpu.VMEM((2, share, features), BF16),
            pltpu.VMEM((2, share, features), BF16),
            dma,
            dma((2,)),
            dma((chunks, PIECES)),
            dma((chunks, PIECES)),
            dma((chunks, PIECES)),
            dma((chunks, PIECES)),
            dma((4, chunks, 3)),
            dma((4, chunks, 3)),
            dma((4,)),
            dma((4,)),
            dma((2, 2)),
            dma((2, 2)),
            dma((2,)),
            dma((2,)),
        ],
        compiler_params=pltpu.CompilerParams(
            collective_id=0, has_side_effects=True, vmem_limit_bytes=56 * 2**20
        ),
    )(
        x0.reshape(act),
        w_key[0],
        w_value[0],
        w_score.reshape(1, model),
        segments,
        lengths,
        grades,
    )
    return (grad_key[None], grad_value[None])


def solution(mesh):
    placed = (
        P(None, "dp", None),
        P("section", None, None),
        P("section", None, None),
        P(),
        P(None, "dp"),
        P(None, "dp"),
        P(None, "dp"),
    )
    return jax.shard_map(
        shards,
        mesh=mesh,
        in_specs=placed,
        out_specs=(P("section", "dp", None), P("section", "dp", None)),
        check_vma=False,
    )
```

```python
import functools
import math

import jax
import jax.numpy as jnp
from jax import lax
from jax.experimental import pallas as pl
from jax.experimental.pallas import tpu as pltpu
from jax.sharding import PartitionSpec as P

HD = 128
HEADS = 4
EPS = 1e-06
THETA = 1000000.0
SUB = 16
PIECES = 4
STRIPS = 5
MESH = pl.DeviceIdType.MESH
F32 = jnp.float32
BF16 = jnp.bfloat16


def dot(left, right):
    return jnp.dot(left, right, preferred_element_type=F32)


def dot_t(left, right):
    return lax.dot_general(left, right, (((1,), (1,)), ((), ())), preferred_element_type=F32)


def t_dot(left, right):
    return lax.dot_general(left, right, (((0,), (0,)), ((), ())), preferred_element_type=F32)


def stack(array):
    blocks = []
    for start in range(0, array.shape[0], SUB):
        blocks += [array[start : start + SUB, h * HD : (h + 1) * HD] for h in range(HEADS)]
    return jnp.concatenate(blocks, axis=0)


def unstack(array):
    rows = []
    for start in range(0, array.shape[0], HEADS * SUB):
        blocks = [array[start + h * SUB : start + (h + 1) * SUB] for h in range(HEADS)]
        rows.append(jnp.concatenate(blocks, axis=1))
    return jnp.concatenate(rows, axis=0)


def swap(array):
    return pltpu.roll(array, HD // 2, 1)


def tall(array):
    return jnp.concatenate([array[k] for k in range(array.shape[0]) for h in range(HEADS)], axis=0)


def pipe_kernel(
    sections,
    x0,
    wk_all,
    wv_all,
    wscore,
    segments,
    lengths,
    grades,
    out_key,
    out_value,
    wk,
    wv,
    wkt,
    wvt,
    slots,
    cosine,
    sine,
    mask,
    ends,
    levels,
    hin,
    gin,
    gkv,
    mixs,
    hout,
    gout,
    keys,
    values,
    probs,
    scales,
    carry_v,
    carry_k,
    peer_h,
    peer_g,
    peer_gkv,
    peer_mix,
    total,
    pair_out,
    pair_in,
    first_out,
    first_in,
    second_out,
    second_in,
    weight_sem,
    hsend,
    hrecv,
    gsend,
    grecv,
    xsend,
    xrecv,
    pair_send,
    pair_recv,
    first_send,
    first_recv,
    second_send,
    second_recv,
):
    section = lax.axis_index("section")
    place = lax.axis_index("dp")
    x, y, core = place // 8, (place // 2) % 4, place % 2
    xpeers = [((x + r) % 4) * 8 + place % 8 for r in range(1, 4)]
    sibling = x * 8 + y * 2 + (1 - core)
    beside = y + 1 - 2 * (y % 2)
    across = 3 - y
    opposite = (y + 2) % 4
    ydevices = [x * 8 + beside * 2 + core, x * 8 + across * 2 + core]
    last = sections - 1
    chunks = hin.shape[0]
    model = hin.shape[2]
    piece = model // PIECES
    strip = model // STRIPS
    up = jnp.minimum(section + 1, last)
    down = jnp.maximum(section - 1, 0)

    rows = HEADS * SUB
    load_k = pltpu.make_async_copy(wk_all, wk, weight_sem.at[0])
    load_v = pltpu.make_async_copy(wv_all, wv, weight_sem.at[1])
    load_k.start()
    load_v.start()

    @pl.when(section == 0)
    def _():
        def load(c, unused):
            for p in range(STRIPS):
                there = pl.ds(p * strip, strip)
                pltpu.make_async_copy(
                    x0.at[c, :, there], hin.at[c, :, there], hrecv.at[c, p]
                ).start()
            return unused

        lax.fori_loop(0, chunks, load, 0)

    barrier = pltpu.get_barrier_semaphore()

    @pl.when(section < last)
    def _():
        pl.semaphore_signal(barrier, inc=1, device_id={"section": up}, device_id_type=MESH)

    @pl.when(section > 0)
    def _():
        pl.semaphore_signal(barrier, inc=1, device_id={"section": down}, device_id_type=MESH)

    for peer in xpeers + ydevices + [sibling]:
        pl.semaphore_signal(barrier, inc=1, device_id={"dp": peer}, device_id_type=MESH)

    keys[...] = jnp.zeros_like(keys)
    values[...] = jnp.zeros_like(values)
    source = lax.broadcasted_iota(jnp.int32, (slots.shape[0] * 4, 2 * rows), 0)
    lane = lax.broadcasted_iota(jnp.int32, (slots.shape[0] * 4, 2 * rows), 1)
    spread = (source == (lane // rows) * SUB + lane % SUB).astype(BF16)
    both = jnp.concatenate([segments[...], grades[...]], axis=0).astype(F32).astype(BF16)
    slots[...] = dot(both, spread)

    def make_tables(c, unused):
        row, half = c // 2, lax.rem(c, 2)
        sub = lax.broadcasted_iota(jnp.int32, (rows, 2 * rows), 0)
        lane = lax.broadcasted_iota(jnp.int32, (rows, 2 * rows), 1)
        slot_i = half * SUB + sub % SUB
        slot_j = (lane // rows) * SUB + lane % SUB
        seg_j = jnp.broadcast_to(slots[pl.ds(row, 1), :], (rows, 2 * rows))
        grade_j = jnp.broadcast_to(slots[pl.ds(row + chunks // 2, 1), :], (rows, 2 * rows))
        here = lane == half * rows + sub
        seg_i = jnp.sum(jnp.where(here, seg_j, 0.0), axis=1, keepdims=True)
        grade_i = jnp.sum(jnp.where(here, grade_j, 0.0), axis=1, keepdims=True)
        entry = lax.broadcasted_iota(jnp.int32, lengths.shape, 1)
        length = jnp.sum(
            jnp.where(entry == row, lengths[...].astype(F32), 0.0), axis=1, keepdims=True
        )
        length = jnp.broadcast_to(length, (rows, 2 * rows)).astype(jnp.int32)
        same = seg_j == seg_i
        live = slot_i < length
        allowed = (same & (slot_j <= slot_i) & live & (slot_j < length)) | (slot_i == slot_j)
        heads = sub // SUB == (lane // SUB) % HEADS
        mask[c] = jnp.where(allowed & heads, 1.0, 0.0)
        once = (lane // SUB) % HEADS == 0
        before = jnp.sum(jnp.where(once & (seg_j < seg_i), 1.0, 0.0), axis=1, keepdims=True)
        after = jnp.sum(
            jnp.where(once & same & (slot_j > slot_i), 1.0, 0.0), axis=1, keepdims=True
        )
        final = (after == 0.0) | (slot_i == length - 1)
        ends[c] = jnp.where(live & final, 1.0, 0.0)[:SUB, :1]
        levels[c] = grade_i[:SUB]
        position = slot_i[:SUB].astype(F32) - before[:SUB]
        lane = lane[:SUB]
        freqs = jnp.exp((lane % (HD // 2)).astype(F32) * (-2.0 * math.log(THETA) / HD))
        angles = position * freqs
        cosine[c] = jnp.cos(angles)
        sine[c] = jnp.where(lane < HD // 2, -1.0, 1.0) * jnp.sin(angles)
        return unused

    lax.fori_loop(0, chunks, make_tables, 0)

    load_k.wait()
    load_v.wait()

    @pl.when((section > 0) & (section < last))
    def _():
        pl.semaphore_wait(barrier, 8)

    @pl.when((section == 0) | (section == last))
    def _():
        pl.semaphore_wait(barrier, 7)

    def turn(source, target):
        def block(t, unused):
            there = pl.ds(pl.multiple_of(t * 256, 256), 256)
            target[:, there] = source[there, :].T
            return unused

        lax.fori_loop(0, model // 256, block, 0)

    @pl.when(section > 0)
    def _():
        turn(wv, wvt)

    @pl.when(section > 1)
    def _():
        turn(wk, wkt)

    def columns(p):
        return pl.ds(p * strip, strip)

    def h_copy(c, p):
        return pltpu.make_async_remote_copy(
            src_ref=hout.at[c, :, columns(p)],
            dst_ref=hin.at[c, :, columns(p)],
            send_sem=hsend.at[c, p],
            recv_sem=hrecv.at[c, p],
            device_id={"section": up},
            device_id_type=MESH,
        )

    def g_copy(c, p):
        return pltpu.make_async_remote_copy(
            src_ref=gout.at[c, :, columns(p)],
            dst_ref=gin.at[c, :, columns(p)],
            send_sem=gsend.at[c, p],
            recv_sem=grecv.at[c, p],
            device_id={"section": down},
            device_id_type=MESH,
        )

    def x_copy(kind, c, r):
        peer = (x + r) % 4
        source, target = (
            (hin.at[c, :, pl.ds(pl.multiple_of(peer * piece, 128), piece)], peer_h),
            (mixs.at[c], peer_mix),
            (gin.at[c, :, pl.ds(pl.multiple_of(peer * piece, 128), piece)], peer_g),
            (gkv.at[c], peer_gkv),
        )[kind]
        return pltpu.make_async_remote_copy(
            src_ref=source,
            dst_ref=target.at[r - 1, c],
            send_sem=xsend.at[kind, c, r - 1],
            recv_sem=xrecv.at[kind, c, r - 1],
            device_id={"dp": xpeers[r - 1]},
            device_id_type=MESH,
        )

    def forward(c, n):
        some = pl.ds(c, n)
        lines = n * SUB
        row = c // 2

        def held(p):
            return hin[some, :, columns(p)].reshape(lines, strip)

        acc_k = jnp.zeros((lines, HEADS * HD), F32)
        acc_v = jnp.zeros((lines, HEADS * HD), F32)
        square = jnp.zeros((lines, 1), F32)
        for p in range(STRIPS):
            for k in range(n):
                h_copy(c + k, p).wait_recv()
            part = held(p)
            acc_k += dot(part, wk[columns(p), :])
            acc_v += dot(part, wv[columns(p), :])
            full = part.astype(F32)
            square += jnp.sum(full * full, axis=1, keepdims=True)
        scale = lax.rsqrt(square / model + EPS)
        scales[some] = scale.reshape(n, SUB, 1)
        turned = stack(acc_k * scale)
        turned = turned * tall(cosine[some]) + swap(turned) * tall(sine[some])
        key = turned.astype(BF16)
        value = stack(acc_v * scale).astype(BF16)
        keys[some] = key.reshape(n, rows, HD)
        values[some] = value.reshape(n, rows, HD)
        all_keys = keys[pl.ds(row * 2, 2)].reshape(2 * rows, HD)
        all_values = values[pl.ds(row * 2, 2)].reshape(2 * rows, HD)
        logits = dot_t(key, all_keys) * (1.0 / HD)
        logits = jnp.where(mask[some].reshape(n * rows, 2 * rows) > 0.0, logits, -1e30)
        top = jnp.max(logits, axis=1, keepdims=True)
        expd = jnp.exp(logits - top)
        prob = expd / jnp.sum(expd, axis=1, keepdims=True)
        probs[some] = prob.reshape(n, rows, 2 * rows)
        mixed = unstack(dot(prob.astype(BF16), all_values).astype(BF16))
        mixs[some] = mixed.reshape(n, SUB, HEADS * HD)

        def output(p, product):
            out = held(p).astype(F32) + product
            hout[some, :, columns(p)] = out.astype(BF16).reshape(n, SUB, strip)

        if n == 1:

            @pl.when(section == 0)
            def _():
                for p in range(STRIPS):
                    output(p, dot_t(mixed, wv[columns(p), :]))
                    h_copy(c, p).start()

            @pl.when(section > 0)
            def _():
                for p in range(STRIPS):
                    output(p, dot(mixed, wvt[:, columns(p)]))
                    h_copy(c, p).start()

        else:
            for p in range(STRIPS):
                output(p, dot(mixed, wvt[:, columns(p)]))

        for k in range(n):
            for r in range(1, 4):
                x_copy(0, c + k, r).start()
                x_copy(1, c + k, r).start()

    def loss(c):
        some = pl.ds(c, 2)
        square = jnp.zeros((2, SUB, 1), F32)
        score = jnp.zeros((2, SUB, 1), F32)
        for p in range(STRIPS):
            full = hout[some, :, columns(p)].astype(F32)
            square += jnp.sum(full * full, axis=2, keepdims=True)
            score += jnp.sum(full * wscore[:, columns(p)][None], axis=2, keepdims=True)
        scale = lax.rsqrt(square / model + EPS)
        score = score * scale
        end = ends[some]

        def softmax(entries):
            masked = jnp.where(end > 0.0, entries, -1e30)
            top = jnp.max(jnp.max(masked, axis=0), axis=0, keepdims=True)
            expd = jnp.where(end > 0.0, jnp.exp(masked - top[None]), 0.0)
            return expd / jnp.sum(jnp.sum(expd, axis=0), axis=0, keepdims=True)[None]

        weight = jnp.where(end > 0.0, softmax(score) - softmax(levels[some]), 0.0)
        first = scale * weight
        second = scale * scale * weight * score * (1.0 / model)
        for p in range(STRIPS):
            full = hout[some, :, columns(p)].astype(F32)
            grad = first * wscore[:, columns(p)][None] - second * full
            gin[some, :, columns(p)] = grad.astype(BF16)

    def backward(c, n):
        some = pl.ds(c, n)
        lines = n * SUB
        row = c // 2

        def grad_at(p):
            return gin[some, :, columns(p)].reshape(lines, strip)

        acc = jnp.zeros((lines, HEADS * HD), F32)
        for p in range(STRIPS):
            if n == 1:
                g_copy(c, p).wait_recv()
            acc += dot(grad_at(p), wv[columns(p), :])
        scale = scales[some].reshape(lines, 1)
        grad_mixed = stack(acc).astype(BF16)
        all_keys = keys[pl.ds(row * 2, 2)].reshape(2 * rows, HD)
        all_values = values[pl.ds(row * 2, 2)].reshape(2 * rows, HD)
        key = keys[some].reshape(n * rows, HD)
        value = values[some].reshape(n * rows, HD)
        prob = probs[some].reshape(n * rows, 2 * rows)
        grad_probs = dot_t(grad_mixed, all_values)
        product = prob * grad_probs
        grad_scores = (product - prob * jnp.sum(product, axis=1, keepdims=True)).astype(BF16)
        own_v = t_dot(prob.astype(BF16), grad_mixed)
        own_k = t_dot(grad_scores, key)
        if n == 1:
            second = lax.rem(c, 2) == 1
            from_v, from_k = own_v, own_k
            own_v = jnp.where(second, from_v[rows:], from_v[:rows] + carry_v[...])
            own_k = jnp.where(second, from_k[rows:], from_k[:rows] + carry_k[...])
            carry_v[...] = from_v[:rows]
            carry_k[...] = from_k[:rows]
        turned = (dot(grad_scores, all_keys) + own_k) * (1.0 / HD)
        along = jnp.sum(turned * key.astype(F32) + own_v * value.astype(F32), axis=1, keepdims=True)
        along = jnp.sum(along.reshape(n, HEADS, SUB, 1), axis=1).reshape(lines, 1)
        along = along * (scale * scale) * (1.0 / model)
        grad_key = turned * tall(cosine[some]) - swap(turned) * tall(sine[some])
        flat_key = unstack(grad_key.astype(BF16))
        flat_value = unstack(own_v.astype(BF16))
        features = HEADS * HD
        key_part = (flat_key.astype(F32) * scale).astype(BF16)
        value_part = (flat_value.astype(F32) * scale).astype(BF16)
        gkv[some, :, :features] = key_part.reshape(n, SUB, features)
        gkv[some, :, features:] = value_part.reshape(n, SUB, features)

        @pl.when(section > 0)
        def _():
            for p in range(STRIPS):
                grad = dot(flat_key, wkt[:, columns(p)]) + dot(flat_value, wvt[:, columns(p)])
                full = hin[some, :, columns(p)].reshape(lines, strip).astype(F32)
                out = grad_at(p).astype(F32) + scale * grad - along * full
                gout[some, :, columns(p)] = out.astype(BF16).reshape(n, SUB, strip)
                g_copy(c + n - 1, p).start()
            if n == 2:
                for p in range(STRIPS):
                    g_copy(c, p).start()

        for k in range(n):
            for r in range(1, 4):
                x_copy(2, c + k, r).start()
                x_copy(3, c + k, r).start()

    tile = 256
    group = chunks // 2

    def weights(base):
        def arrive(c, unused):
            for kind in range(4):
                for r in range(1, 4):
                    x_copy(kind, base + c, r).wait_recv()
            return unused

        lax.fori_loop(0, group, arrive, 0)
        which = pl.ds(base, group)

        def gather(own, peers):
            own = own.reshape(group * SUB, own.shape[-1])
            peers = peers.reshape(3 * group * SUB, peers.shape[-1])
            return jnp.concatenate([own, peers], axis=0)

        def block(t, unused):
            there = pl.ds(pl.multiple_of(t * tile, tile), tile)
            mine = pl.ds(pl.multiple_of(x * piece + t * tile, 128), tile)
            hidden = gather(hin[which, :, mine], peer_h[:, which, :, there])
            grads = gather(gin[which, :, mine], peer_g[:, which, :, there])
            both = gather(gkv[which], peer_gkv[:, which])
            mixed = gather(mixs[which], peer_mix[:, which])
            features = HEADS * HD
            part_key = t_dot(hidden, both[:, :features])
            part_value = t_dot(hidden, both[:, features:]) + t_dot(grads, mixed)

            @pl.when(base == 0)
            def _():
                total[there, :features] = part_key
                total[there, features:] = part_value

            @pl.when(base > 0)
            def _():
                total[there, :features] = part_key + total[there, :features]
                total[there, features:] = part_value + total[there, features:]

            return unused

        lax.fori_loop(0, piece // tile, block, 0)

    share = piece // 8
    half_features = HEADS * HD
    sides = [pl.ds(0, half_features), pl.ds(half_features, half_features)]

    def rows_of(ypart, corepart):
        return pl.ds(pl.multiple_of((ypart * 2 + corepart) * share, 32), share)

    def pair_copy(k):
        return pltpu.make_async_remote_copy(
            src_ref=pair_out.at[k],
            dst_ref=pair_in.at[k],
            send_sem=pair_send.at[k],
            recv_sem=pair_recv.at[k],
            device_id={"dp": sibling},
            device_id_type=MESH,
        )

    def first_copy(side, k):
        return pltpu.make_async_remote_copy(
            src_ref=first_out.at[side, k],
            dst_ref=first_in.at[side, k],
            send_sem=first_send.at[side, k],
            recv_sem=first_recv.at[side, k],
            device_id={"dp": ydevices[side]},
            device_id_type=MESH,
        )

    def second_copy(side):
        return pltpu.make_async_remote_copy(
            src_ref=second_out.at[side],
            dst_ref=second_in.at[side],
            send_sem=second_send.at[side],
            recv_sem=second_recv.at[side],
            device_id={"dp": ydevices[1 - side]},
            device_id_type=MESH,
        )

    def scatter():
        order = [opposite, beside, across, y]
        for k in range(4):
            pair_out[k] = total[rows_of(order[k], 1 - core), :].astype(BF16)
            pair_copy(k).start()

        def held(k, side):
            return total[rows_of(order[k], core), sides[side]] + pair_in[k, :, sides[side]].astype(F32)

        pair_copy(0).wait_recv()
        for side in range(2):
            first_out[side, 1] = held(0, side).astype(BF16)
            first_copy(side, 1).start()
        for side in range(2):
            pair_copy(1 + side).wait_recv()
            first_out[side, 0] = held(1 + side, side).astype(BF16)
            first_copy(side, 0).start()
        for side in range(2):
            first_copy(side, 1).wait_recv()
            second_out[side] = (held(2 - side, side) + first_in[side, 1].astype(F32)).astype(BF16)
            second_copy(side).start()
        pair_copy(3).wait_recv()
        for side, out in ((0, out_key), (1, out_value)):
            first_copy(side, 0).wait_recv()
            second_copy(side).wait_recv()
            out[...] = held(3, side) + first_in[side, 0].astype(F32) + second_in[side].astype(F32)
        for k in range(4):
            pair_copy(k).wait_send()
        for side in range(2):
            first_copy(side, 0).wait_send()
            first_copy(side, 1).wait_send()
            second_copy(side).wait_send()

    lead = jnp.where(section == last - 1, 5, chunks)

    def slot(i, unused):
        @pl.when(i < chunks)
        def _():
            forward(i, 1)

        j = i - lead

        @pl.when((j == 0) & (section == 1))
        def _():
            turn(wk, wkt)

        @pl.when((j >= 0) & (j < chunks))
        def _():
            backward((j // 2) * 2 + 1 - lax.rem(j, 2), 1)

        @pl.when((j == group + 1) & (section == 0))
        def _():
            weights(0)

        return unused

    def whole(row, unused):
        forward(row * 2, 2)
        loss(row * 2)
        backward(row * 2, 2)
        return unused

    @pl.when(section < last)
    def _():
        lax.fori_loop(0, 2 * chunks, slot, 0)

    @pl.when(section == last)
    def _():
        lax.fori_loop(0, chunks // 2, whole, 0)

    def rest(step, unused):
        weights(step * group)
        return unused

    lax.fori_loop(jnp.where(section == 0, 1, 0), 2, rest, 0)
    scatter()

    def drain(c, unused):
        for p in range(STRIPS):

            @pl.when(section < last)
            def _():
                h_copy(c, p).wait_send()

            @pl.when(section > 0)
            def _():
                g_copy(c, p).wait_send()

        for kind in range(4):
            for r in range(1, 4):
                x_copy(kind, c, r).wait_send()
        return unused

    lax.fori_loop(0, chunks, drain, 0)


def finish_kernel(key_in, value_in, key_out, value_out):
    key_out[0] = key_in[...]
    value_out[0] = value_in[...]


def shards(x0, w_key, w_value, w_score, segments, lengths, grades):
    sections = lax.axis_size("section")
    micro, width, model = x0.shape
    features = w_key.shape[2]
    chunks = micro * width // SUB
    vmem = pl.BlockSpec(memory_space=pltpu.VMEM)
    act = (chunks, SUB, model)
    flat = (chunks, SUB, features)
    stacked = (chunks, HEADS * SUB, HD)
    piece = model // PIECES
    share = piece // 8
    dma = pltpu.SemaphoreType.DMA
    grad_key, grad_value = pl.pallas_call(
        functools.partial(pipe_kernel, sections),
        out_shape=[jax.ShapeDtypeStruct((share, features), F32)] * 2,
        in_specs=[pl.BlockSpec(memory_space=pl.ANY)] * 3 + [vmem] * 4,
        out_specs=[vmem] * 2,
        scratch_shapes=[
            pltpu.VMEM((model, features), BF16),
            pltpu.VMEM((model, features), BF16),
            pltpu.VMEM((features, model), BF16),
            pltpu.VMEM((features, model), BF16),
            pltpu.VMEM((2 * micro, HD), F32),
            pltpu.VMEM((chunks, SUB, HD), F32),
            pltpu.VMEM((chunks, SUB, HD), F32),
            pltpu.VMEM((chunks, HEADS * SUB, 2 * HEADS * SUB), F32),
            pltpu.VMEM((chunks, SUB, 1), F32),
            pltpu.VMEM((chunks, SUB, 1), F32),
            pltpu.VMEM(act, BF16),
            pltpu.VMEM(act, BF16),
            pltpu.VMEM((chunks, SUB, 2 * features), BF16),
            pltpu.VMEM(flat, BF16),
            pltpu.VMEM(act, BF16),
            pltpu.VMEM(act, BF16),
            pltpu.VMEM(stacked, BF16),
            pltpu.VMEM(stacked, BF16),
            pltpu.VMEM((chunks, HEADS * SUB, 2 * HEADS * SUB), F32),
            pltpu.VMEM((chunks, SUB, 1), F32),
            pltpu.VMEM((HEADS * SUB, HD), F32),
            pltpu.VMEM((HEADS * SUB, HD), F32),
            pltpu.VMEM((3, chunks, SUB, piece), BF16),
            pltpu.VMEM((3, chunks, SUB, piece), BF16),
            pltpu.VMEM((3, chunks, SUB, 2 * features), BF16),
            pltpu.VMEM((3, chunks, SUB, features), BF16),
            pltpu.VMEM((piece, 2 * features), F32),
            pltpu.VMEM((4, share, 2 * features), BF16),
            pltpu.VMEM((4, share, 2 * features), BF16),
            pltpu.VMEM((2, 2, share, features), BF16),
            pltpu.VMEM((2, 2, share, features), BF16),
            pltpu.VMEM((2, share, features), BF16),
            pltpu.VMEM((2, share, features), BF16),
            dma((2,)),
            dma((chunks, STRIPS)),
            dma((chunks, STRIPS)),
            dma((chunks, STRIPS)),
            dma((chunks, STRIPS)),
            dma((4, chunks, 3)),
            dma((4, chunks, 3)),
            dma((4,)),
            dma((4,)),
            dma((2, 2)),
            dma((2, 2)),
            dma((2,)),
            dma((2,)),
        ],
        compiler_params=pltpu.CompilerParams(
            collective_id=0, has_side_effects=True, vmem_limit_bytes=56 * 2**20
        ),
    )(
        x0.reshape(act),
        w_key[0],
        w_value[0],
        w_score.reshape(1, model),
        segments,
        lengths.reshape(1, micro),
        grades,
    )
    grad_key, grad_value = pl.pallas_call(
        finish_kernel,
        out_shape=[jax.ShapeDtypeStruct((1, share, features), F32)] * 2,
        in_specs=[vmem] * 2,
        out_specs=[vmem] * 2,
    )(grad_key, grad_value)
    return (grad_key, grad_value)


def solution(mesh):
    placed = (
        P(None, "dp", None),
        P("section", None, None),
        P("section", None, None),
        P(),
        P(None, "dp"),
        P(None, "dp"),
        P(None, "dp"),
    )
    return jax.shard_map(
        shards,
        mesh=mesh,
        in_specs=placed,
        out_specs=(P("section", "dp", None), P("section", "dp", None)),
        check_vma=False,
    )
```

```python
import functools
import math

import jax
import jax.numpy as jnp
from jax import lax
from jax.experimental import pallas as pl
from jax.experimental.pallas import tpu as pltpu
from jax.sharding import PartitionSpec as P

HD = 128
HEADS = 4
EPS = 1e-06
THETA = 1000000.0
SUB = 16
PIECES = 4
BOUNDS = (0, 1024, 2048, 3072, 4096, 5120)
STRIPS = len(BOUNDS) - 1
MESH = pl.DeviceIdType.MESH
F32 = jnp.float32
BF16 = jnp.bfloat16


def dot(left, right):
    return jnp.dot(left, right, preferred_element_type=F32)


def dot_t(left, right):
    return lax.dot_general(left, right, (((1,), (1,)), ((), ())), preferred_element_type=F32)


def t_dot(left, right):
    return lax.dot_general(left, right, (((0,), (0,)), ((), ())), preferred_element_type=F32)


def stack(array):
    blocks = []
    for start in range(0, array.shape[0], SUB):
        blocks += [array[start : start + SUB, h * HD : (h + 1) * HD] for h in range(HEADS)]
    return jnp.concatenate(blocks, axis=0)


def unstack(array):
    rows = []
    for start in range(0, array.shape[0], HEADS * SUB):
        blocks = [array[start + h * SUB : start + (h + 1) * SUB] for h in range(HEADS)]
        rows.append(jnp.concatenate(blocks, axis=1))
    return jnp.concatenate(rows, axis=0)


def swap(array):
    return pltpu.roll(array, HD // 2, 1)


def tall(array):
    return jnp.concatenate([array[k] for k in range(array.shape[0]) for h in range(HEADS)], axis=0)


def ahead(compute, finish):
    finish(0, compute(0))
    waiting = compute(1)
    for p in range(2, STRIPS):
        following = compute(p)
        finish(p - 1, waiting)
        waiting = following
    finish(STRIPS - 1, waiting)


def pipe_kernel(
    sections,
    x0,
    wk_all,
    wv_all,
    wscore,
    segments,
    lengths,
    grades,
    out_key,
    out_value,
    wk,
    wv,
    wkt,
    wvt,
    slots,
    cosine,
    sine,
    mask,
    ends,
    levels,
    hin,
    gin,
    gkv,
    mixs,
    hout,
    gout,
    keys,
    values,
    probs,
    scales,
    carry_v,
    carry_k,
    peer_h,
    peer_g,
    peer_gkv,
    peer_mix,
    total,
    pair_out,
    pair_in,
    first_out,
    first_in,
    second_out,
    second_in,
    weight_sem,
    hsend,
    hrecv,
    gsend,
    grecv,
    xsend,
    xrecv,
    pair_send,
    pair_recv,
    first_send,
    first_recv,
    second_send,
    second_recv,
):
    section = lax.axis_index("section")
    place = lax.axis_index("dp")
    x, y, core = place // 8, (place // 2) % 4, place % 2
    xpeers = [((x + r) % 4) * 8 + place % 8 for r in range(1, 4)]
    sibling = x * 8 + y * 2 + (1 - core)
    beside = y + 1 - 2 * (y % 2)
    across = 3 - y
    opposite = (y + 2) % 4
    ydevices = [x * 8 + beside * 2 + core, x * 8 + across * 2 + core]
    last = sections - 1
    chunks = hin.shape[0]
    model = hin.shape[2]
    piece = model // PIECES
    up = jnp.minimum(section + 1, last)
    down = jnp.maximum(section - 1, 0)

    def columns(p):
        return pl.ds(BOUNDS[p], BOUNDS[p + 1] - BOUNDS[p])

    rows = HEADS * SUB
    def load_weight(p):
        there = columns(p)
        return [
            pltpu.make_async_copy(source.at[there], target.at[there], weight_sem.at[k, p])
            for k, source, target in ((0, wk_all, wk), (1, wv_all, wv))
        ]

    for p in range(STRIPS):
        for copy in load_weight(p):
            copy.start()

    @pl.when(section == 0)
    def _():
        def load(c, unused):
            for p in range(STRIPS):
                there = columns(p)
                pltpu.make_async_copy(
                    x0.at[c, :, there], hin.at[c, :, there], hrecv.at[c, p]
                ).start()
            return unused

        lax.fori_loop(0, chunks, load, 0)

    barrier = pltpu.get_barrier_semaphore()

    @pl.when(section < last)
    def _():
        pl.semaphore_signal(barrier, inc=1, device_id={"section": up}, device_id_type=MESH)

    @pl.when(section > 0)
    def _():
        pl.semaphore_signal(barrier, inc=1, device_id={"section": down}, device_id_type=MESH)

    for peer in xpeers + ydevices + [sibling]:
        pl.semaphore_signal(barrier, inc=1, device_id={"dp": peer}, device_id_type=MESH)

    keys[...] = jnp.zeros_like(keys)
    values[...] = jnp.zeros_like(values)
    source = lax.broadcasted_iota(jnp.int32, (slots.shape[0] * 4, 2 * rows), 0)
    lane = lax.broadcasted_iota(jnp.int32, (slots.shape[0] * 4, 2 * rows), 1)
    spread = (source == (lane // rows) * SUB + lane % SUB).astype(BF16)
    both = jnp.concatenate([segments[...], grades[...]], axis=0).astype(F32).astype(BF16)
    slots[...] = dot(both, spread)

    def make_tables(c, unused):
        row, half = c // 2, lax.rem(c, 2)
        sub = lax.broadcasted_iota(jnp.int32, (rows, 2 * rows), 0)
        lane = lax.broadcasted_iota(jnp.int32, (rows, 2 * rows), 1)
        slot_i = half * SUB + sub % SUB
        slot_j = (lane // rows) * SUB + lane % SUB
        seg_j = jnp.broadcast_to(slots[pl.ds(row, 1), :], (rows, 2 * rows))
        grade_j = jnp.broadcast_to(slots[pl.ds(row + chunks // 2, 1), :], (rows, 2 * rows))
        here = lane == half * rows + sub
        seg_i = jnp.sum(jnp.where(here, seg_j, 0.0), axis=1, keepdims=True)
        grade_i = jnp.sum(jnp.where(here, grade_j, 0.0), axis=1, keepdims=True)
        entry = lax.broadcasted_iota(jnp.int32, lengths.shape, 1)
        length = jnp.sum(
            jnp.where(entry == row, lengths[...].astype(F32), 0.0), axis=1, keepdims=True
        )
        length = jnp.broadcast_to(length, (rows, 2 * rows)).astype(jnp.int32)
        same = seg_j == seg_i
        live = slot_i < length
        allowed = (same & (slot_j <= slot_i) & live & (slot_j < length)) | (slot_i == slot_j)
        heads = sub // SUB == (lane // SUB) % HEADS
        mask[c] = jnp.where(allowed & heads, 1.0, 0.0)
        once = (lane // SUB) % HEADS == 0
        before = jnp.sum(jnp.where(once & (seg_j < seg_i), 1.0, 0.0), axis=1, keepdims=True)
        after = jnp.sum(
            jnp.where(once & same & (slot_j > slot_i), 1.0, 0.0), axis=1, keepdims=True
        )
        final = (after == 0.0) | (slot_i == length - 1)
        ends[c] = jnp.where(live & final, 1.0, 0.0)[:SUB, :1]
        levels[c] = grade_i[:SUB]
        position = slot_i[:SUB].astype(F32) - before[:SUB]
        lane = lane[:SUB]
        freqs = jnp.exp((lane % (HD // 2)).astype(F32) * (-2.0 * math.log(THETA) / HD))
        angles = position * freqs
        cosine[c] = jnp.cos(angles)
        sine[c] = jnp.where(lane < HD // 2, -1.0, 1.0) * jnp.sin(angles)
        return unused

    lax.fori_loop(0, chunks, make_tables, 0)

    @pl.when(section > 0)
    def _():
        for p in range(STRIPS):
            for copy in load_weight(p):
                copy.wait()

    @pl.when((section > 0) & (section < last))
    def _():
        pl.semaphore_wait(barrier, 8)

    @pl.when((section == 0) | (section == last))
    def _():
        pl.semaphore_wait(barrier, 7)

    def turn(source, target):
        def block(t, unused):
            there = pl.ds(pl.multiple_of(t * 256, 256), 256)
            target[:, there] = source[there, :].T
            return unused

        lax.fori_loop(0, model // 256, block, 0)

    @pl.when(section > 0)
    def _():
        turn(wv, wvt)

    @pl.when(section > 1)
    def _():
        turn(wk, wkt)

    def h_copy(c, p):
        return pltpu.make_async_remote_copy(
            src_ref=hout.at[c, :, columns(p)],
            dst_ref=hin.at[c, :, columns(p)],
            send_sem=hsend.at[c, p],
            recv_sem=hrecv.at[c, p],
            device_id={"section": up},
            device_id_type=MESH,
        )

    def g_copy(c, p):
        return pltpu.make_async_remote_copy(
            src_ref=gout.at[c, :, columns(p)],
            dst_ref=gin.at[c, :, columns(p)],
            send_sem=gsend.at[c, p],
            recv_sem=grecv.at[c, p],
            device_id={"section": down},
            device_id_type=MESH,
        )

    def x_copy(kind, c, r):
        peer = (x + r) % 4
        source, target = (
            (hin.at[c, :, pl.ds(pl.multiple_of(peer * piece, 128), piece)], peer_h),
            (mixs.at[c], peer_mix),
            (gin.at[c, :, pl.ds(pl.multiple_of(peer * piece, 128), piece)], peer_g),
            (gkv.at[c], peer_gkv),
        )[kind]
        return pltpu.make_async_remote_copy(
            src_ref=source,
            dst_ref=target.at[r - 1, c],
            send_sem=xsend.at[kind, c, r - 1],
            recv_sem=xrecv.at[kind, c, r - 1],
            device_id={"dp": xpeers[r - 1]},
            device_id_type=MESH,
        )

    def forward(c, n):
        some = pl.ds(c, n)
        lines = n * SUB
        row = c // 2

        def held(p):
            part = hin[some, :, columns(p)]
            return part.reshape(lines, part.shape[-1])

        acc_k = jnp.zeros((lines, HEADS * HD), F32)
        acc_v = jnp.zeros((lines, HEADS * HD), F32)
        square = jnp.zeros((lines, 1), F32)
        for p in range(STRIPS):
            for k in range(n):
                h_copy(c + k, p).wait_recv()
            if n == 1:

                @pl.when((section == 0) & (c == 0))
                def _():
                    for copy in load_weight(p):
                        copy.wait()

            part = held(p)
            acc_k += dot(part, wk[columns(p), :])
            acc_v += dot(part, wv[columns(p), :])
            full = part.astype(F32)
            square += jnp.sum(full * full, axis=1, keepdims=True)
        scale = lax.rsqrt(square / model + EPS)
        scales[some] = scale.reshape(n, SUB, 1)
        turned = stack(acc_k * scale)
        turned = turned * tall(cosine[some]) + swap(turned) * tall(sine[some])
        key = turned.astype(BF16)
        value = stack(acc_v * scale).astype(BF16)
        keys[some] = key.reshape(n, rows, HD)
        values[some] = value.reshape(n, rows, HD)
        all_keys = keys[pl.ds(row * 2, 2)].reshape(2 * rows, HD)
        all_values = values[pl.ds(row * 2, 2)].reshape(2 * rows, HD)
        logits = dot_t(key, all_keys) * (1.0 / HD)
        logits = jnp.where(mask[some].reshape(n * rows, 2 * rows) > 0.0, logits, -1e30)
        top = jnp.max(logits, axis=1, keepdims=True)
        expd = jnp.exp(logits - top)
        prob = expd / jnp.sum(expd, axis=1, keepdims=True)
        probs[some] = prob.reshape(n, rows, 2 * rows)
        mixed = unstack(dot(prob.astype(BF16), all_values).astype(BF16))
        mixs[some] = mixed.reshape(n, SUB, HEADS * HD)

        def strip_of(p, product):
            return (held(p).astype(F32) + product).astype(BF16).reshape(n, SUB, -1)

        def send(p, out):
            hout[some, :, columns(p)] = out
            if n == 1:
                h_copy(c, p).start()

        if n == 1:

            @pl.when(section == 0)
            def _():
                ahead(lambda p: strip_of(p, dot_t(mixed, wv[columns(p), :])), send)

            @pl.when(section > 0)
            def _():
                ahead(lambda p: strip_of(p, dot(mixed, wvt[:, columns(p)])), send)

        else:
            ahead(lambda p: strip_of(p, dot(mixed, wvt[:, columns(p)])), send)

        for k in range(n):
            for r in range(1, 4):
                x_copy(0, c + k, r).start()
                x_copy(1, c + k, r).start()

    def loss(c):
        some = pl.ds(c, 2)
        square = jnp.zeros((2, SUB, 1), F32)
        score = jnp.zeros((2, SUB, 1), F32)
        for p in range(STRIPS):
            full = hout[some, :, columns(p)].astype(F32)
            square += jnp.sum(full * full, axis=2, keepdims=True)
            score += jnp.sum(full * wscore[:, columns(p)][None], axis=2, keepdims=True)
        scale = lax.rsqrt(square / model + EPS)
        score = score * scale
        end = ends[some]

        def softmax(entries):
            masked = jnp.where(end > 0.0, entries, -1e30)
            top = jnp.max(jnp.max(masked, axis=0), axis=0, keepdims=True)
            expd = jnp.where(end > 0.0, jnp.exp(masked - top[None]), 0.0)
            return expd / jnp.sum(jnp.sum(expd, axis=0), axis=0, keepdims=True)[None]

        weight = jnp.where(end > 0.0, softmax(score) - softmax(levels[some]), 0.0)
        first = scale * weight
        second = scale * scale * weight * score * (1.0 / model)
        for p in range(STRIPS):
            full = hout[some, :, columns(p)].astype(F32)
            grad = first * wscore[:, columns(p)][None] - second * full
            gin[some, :, columns(p)] = grad.astype(BF16)

    def backward(c, n):
        some = pl.ds(c, n)
        lines = n * SUB
        row = c // 2

        def grad_at(p):
            part = gin[some, :, columns(p)]
            return part.reshape(lines, part.shape[-1])

        acc = jnp.zeros((lines, HEADS * HD), F32)
        for p in range(STRIPS):
            if n == 1:
                g_copy(c, p).wait_recv()
            acc += dot(grad_at(p), wv[columns(p), :])
        scale = scales[some].reshape(lines, 1)
        grad_mixed = stack(acc).astype(BF16)
        all_keys = keys[pl.ds(row * 2, 2)].reshape(2 * rows, HD)
        all_values = values[pl.ds(row * 2, 2)].reshape(2 * rows, HD)
        key = keys[some].reshape(n * rows, HD)
        value = values[some].reshape(n * rows, HD)
        prob = probs[some].reshape(n * rows, 2 * rows)
        grad_probs = dot_t(grad_mixed, all_values)
        product = prob * grad_probs
        grad_scores = (product - prob * jnp.sum(product, axis=1, keepdims=True)).astype(BF16)
        own_v = t_dot(prob.astype(BF16), grad_mixed)
        own_k = t_dot(grad_scores, key)
        if n == 1:
            second = lax.rem(c, 2) == 1
            from_v, from_k = own_v, own_k
            own_v = jnp.where(second, from_v[rows:], from_v[:rows] + carry_v[...])
            own_k = jnp.where(second, from_k[rows:], from_k[:rows] + carry_k[...])
            carry_v[...] = from_v[:rows]
            carry_k[...] = from_k[:rows]
        turned = (dot(grad_scores, all_keys) + own_k) * (1.0 / HD)
        along = jnp.sum(turned * key.astype(F32) + own_v * value.astype(F32), axis=1, keepdims=True)
        along = jnp.sum(along.reshape(n, HEADS, SUB, 1), axis=1).reshape(lines, 1)
        along = along * (scale * scale) * (1.0 / model)
        grad_key = turned * tall(cosine[some]) - swap(turned) * tall(sine[some])
        flat_key = unstack(grad_key.astype(BF16))
        flat_value = unstack(own_v.astype(BF16))
        features = HEADS * HD
        key_part = (flat_key.astype(F32) * scale).astype(BF16)
        value_part = (flat_value.astype(F32) * scale).astype(BF16)
        gkv[some, :, :features] = key_part.reshape(n, SUB, features)
        gkv[some, :, features:] = value_part.reshape(n, SUB, features)

        @pl.when(section > 0)
        def _():
            def strip_of(p):
                grad = dot(flat_key, wkt[:, columns(p)]) + dot(flat_value, wvt[:, columns(p)])
                full = hin[some, :, columns(p)].reshape(lines, -1).astype(F32)
                out = grad_at(p).astype(F32) + scale * grad - along * full
                return out.astype(BF16).reshape(n, SUB, -1)

            def send(p, out):
                gout[some, :, columns(p)] = out
                g_copy(c + n - 1, p).start()

            ahead(strip_of, send)
            if n == 2:
                for p in range(STRIPS):
                    g_copy(c, p).start()

        for k in range(n):
            for r in range(1, 4):
                x_copy(2, c + k, r).start()
                x_copy(3, c + k, r).start()

    tile = 256
    group = chunks // 2

    share = piece // 8
    half_features = HEADS * HD
    sides = [pl.ds(0, half_features), pl.ds(half_features, half_features)]

    def rows_of(ypart, corepart):
        return pl.ds(pl.multiple_of((ypart * 2 + corepart) * share, 32), share)

    def pair_copy(k):
        return pltpu.make_async_remote_copy(
            src_ref=pair_out.at[k],
            dst_ref=pair_in.at[k],
            send_sem=pair_send.at[k],
            recv_sem=pair_recv.at[k],
            device_id={"dp": sibling},
            device_id_type=MESH,
        )

    def weights(base):
        def arrive(c, unused):
            for kind in range(4):
                for r in range(1, 4):
                    x_copy(kind, base + c, r).wait_recv()
            return unused

        lax.fori_loop(0, group, arrive, 0)
        which = pl.ds(base, group)

        def gather(own, peers):
            own = own.reshape(group * SUB, own.shape[-1])
            peers = peers.reshape(3 * group * SUB, peers.shape[-1])
            return jnp.concatenate([own, peers], axis=0)

        def block(t, unused):
            there = pl.ds(pl.multiple_of(t * tile, tile), tile)
            mine = pl.ds(pl.multiple_of(x * piece + t * tile, 128), tile)
            hidden = gather(hin[which, :, mine], peer_h[:, which, :, there])
            grads = gather(gin[which, :, mine], peer_g[:, which, :, there])
            both = gather(gkv[which], peer_gkv[:, which])
            mixed = gather(mixs[which], peer_mix[:, which])
            features = HEADS * HD
            part_key = t_dot(hidden, both[:, :features])
            part_value = t_dot(hidden, both[:, features:]) + t_dot(grads, mixed)

            @pl.when(base == 0)
            def _():
                total[there, :features] = part_key
                total[there, features:] = part_value

            @pl.when(base > 0)
            def _():
                total[there, :features] = part_key + total[there, :features]
                total[there, features:] = part_value + total[there, features:]

            for k in range(4):
                ready = ((k * 2 + 2 - core) * share + tile - 1) // tile - 1

                @pl.when((base > 0) & (t == ready))
                def _():
                    pair_out[k] = total[rows_of(k, 1 - core), :].astype(BF16)
                    pair_copy(k).start()

            return unused

        lax.fori_loop(0, piece // tile, block, 0)

    def first_copy(side, k):
        return pltpu.make_async_remote_copy(
            src_ref=first_out.at[side, k],
            dst_ref=first_in.at[side, k],
            send_sem=first_send.at[side, k],
            recv_sem=first_recv.at[side, k],
            device_id={"dp": ydevices[side]},
            device_id_type=MESH,
        )

    def second_copy(side):
        return pltpu.make_async_remote_copy(
            src_ref=second_out.at[side],
            dst_ref=second_in.at[side],
            send_sem=second_send.at[side],
            recv_sem=second_recv.at[side],
            device_id={"dp": ydevices[1 - side]},
            device_id_type=MESH,
        )

    def scatter():
        order = [opposite, beside, across, y]
        for k in range(4):
            pair_copy(k).wait_recv()

        def held(k, side):
            other = pair_in[order[k], :, sides[side]].astype(F32)
            return total[rows_of(order[k], core), sides[side]] + other

        for side in range(2):
            first_out[side, 1] = held(0, side).astype(BF16)
            first_copy(side, 1).start()
        for side in range(2):
            first_out[side, 0] = held(1 + side, side).astype(BF16)
            first_copy(side, 0).start()
        for side in range(2):
            first_copy(side, 1).wait_recv()
            second_out[side] = (held(2 - side, side) + first_in[side, 1].astype(F32)).astype(BF16)
            second_copy(side).start()
        for side, out in ((0, out_key), (1, out_value)):
            first_copy(side, 0).wait_recv()
            second_copy(side).wait_recv()
            out[...] = held(3, side) + first_in[side, 0].astype(F32) + second_in[side].astype(F32)
        for k in range(4):
            pair_copy(k).wait_send()
        for side in range(2):
            first_copy(side, 0).wait_send()
            first_copy(side, 1).wait_send()
            second_copy(side).wait_send()

    lead = jnp.where(section == last - 1, 5, chunks)

    def slot(i, unused):
        @pl.when(i < chunks)
        def _():
            forward(i, 1)

        j = i - lead

        @pl.when((j == 0) & (section == 1))
        def _():
            turn(wk, wkt)

        @pl.when((j >= 0) & (j < chunks))
        def _():
            backward((j // 2) * 2 + 1 - lax.rem(j, 2), 1)

        @pl.when((j == group + 1) & (section == 0))
        def _():
            weights(0)

        return unused

    def whole(row, unused):
        forward(row * 2, 2)
        loss(row * 2)
        backward(row * 2, 2)
        return unused

    @pl.when(section < last)
    def _():
        lax.fori_loop(0, 2 * chunks, slot, 0)

    @pl.when(section == last)
    def _():
        lax.fori_loop(0, chunks // 2, whole, 0)

    def rest(step, unused):
        weights(step * group)
        return unused

    lax.fori_loop(jnp.where(section == 0, 1, 0), 2, rest, 0)
    scatter()

    def drain(c, unused):
        for p in range(STRIPS):

            @pl.when(section < last)
            def _():
                h_copy(c, p).wait_send()

            @pl.when(section > 0)
            def _():
                g_copy(c, p).wait_send()

        for kind in range(4):
            for r in range(1, 4):
                x_copy(kind, c, r).wait_send()
        return unused

    lax.fori_loop(0, chunks, drain, 0)


def finish_kernel(key_in, value_in, key_out, value_out):
    key_out[0] = key_in[...]
    value_out[0] = value_in[...]


def shards(x0, w_key, w_value, w_score, segments, lengths, grades):
    sections = lax.axis_size("section")
    micro, width, model = x0.shape
    features = w_key.shape[2]
    chunks = micro * width // SUB
    vmem = pl.BlockSpec(memory_space=pltpu.VMEM)
    act = (chunks, SUB, model)
    flat = (chunks, SUB, features)
    stacked = (chunks, HEADS * SUB, HD)
    piece = model // PIECES
    share = piece // 8
    dma = pltpu.SemaphoreType.DMA
    grad_key, grad_value = pl.pallas_call(
        functools.partial(pipe_kernel, sections),
        out_shape=[jax.ShapeDtypeStruct((share, features), F32)] * 2,
        in_specs=[pl.BlockSpec(memory_space=pl.ANY)] * 3 + [vmem] * 4,
        out_specs=[vmem] * 2,
        scratch_shapes=[
            pltpu.VMEM((model, features), BF16),
            pltpu.VMEM((model, features), BF16),
            pltpu.VMEM((features, model), BF16),
            pltpu.VMEM((features, model), BF16),
            pltpu.VMEM((2 * micro, HD), F32),
            pltpu.VMEM((chunks, SUB, HD), F32),
            pltpu.VMEM((chunks, SUB, HD), F32),
            pltpu.VMEM((chunks, HEADS * SUB, 2 * HEADS * SUB), F32),
            pltpu.VMEM((chunks, SUB, 1), F32),
            pltpu.VMEM((chunks, SUB, 1), F32),
            pltpu.VMEM(act, BF16),
            pltpu.VMEM(act, BF16),
            pltpu.VMEM((chunks, SUB, 2 * features), BF16),
            pltpu.VMEM(flat, BF16),
            pltpu.VMEM(act, BF16),
            pltpu.VMEM(act, BF16),
            pltpu.VMEM(stacked, BF16),
            pltpu.VMEM(stacked, BF16),
            pltpu.VMEM((chunks, HEADS * SUB, 2 * HEADS * SUB), F32),
            pltpu.VMEM((chunks, SUB, 1), F32),
            pltpu.VMEM((HEADS * SUB, HD), F32),
            pltpu.VMEM((HEADS * SUB, HD), F32),
            pltpu.VMEM((3, chunks, SUB, piece), BF16),
            pltpu.VMEM((3, chunks, SUB, piece), BF16),
            pltpu.VMEM((3, chunks, SUB, 2 * features), BF16),
            pltpu.VMEM((3, chunks, SUB, features), BF16),
            pltpu.VMEM((piece, 2 * features), F32),
            pltpu.VMEM((4, share, 2 * features), BF16),
            pltpu.VMEM((4, share, 2 * features), BF16),
            pltpu.VMEM((2, 2, share, features), BF16),
            pltpu.VMEM((2, 2, share, features), BF16),
            pltpu.VMEM((2, share, features), BF16),
            pltpu.VMEM((2, share, features), BF16),
            dma((2, STRIPS)),
            dma((chunks, STRIPS)),
            dma((chunks, STRIPS)),
            dma((chunks, STRIPS)),
            dma((chunks, STRIPS)),
            dma((4, chunks, 3)),
            dma((4, chunks, 3)),
            dma((4,)),
            dma((4,)),
            dma((2, 2)),
            dma((2, 2)),
            dma((2,)),
            dma((2,)),
        ],
        compiler_params=pltpu.CompilerParams(
            collective_id=0, has_side_effects=True, vmem_limit_bytes=56 * 2**20
        ),
    )(
        x0.reshape(act),
        w_key[0],
        w_value[0],
        w_score.reshape(1, model),
        segments,
        lengths.reshape(1, micro),
        grades,
    )
    grad_key, grad_value = pl.pallas_call(
        finish_kernel,
        out_shape=[jax.ShapeDtypeStruct((1, share, features), F32)] * 2,
        in_specs=[vmem] * 2,
        out_specs=[vmem] * 2,
    )(grad_key, grad_value)
    return (grad_key, grad_value)


def solution(mesh):
    placed = (
        P(None, "dp", None),
        P("section", None, None),
        P("section", None, None),
        P(),
        P(None, "dp"),
        P(None, "dp"),
        P(None, "dp"),
    )
    return jax.shard_map(
        shards,
        mesh=mesh,
        in_specs=placed,
        out_specs=(P("section", "dp", None), P("section", "dp", None)),
        check_vma=False,
    )
```

```python
import functools
import math

import jax
import jax.numpy as jnp
from jax import lax
from jax.experimental import pallas as pl
from jax.experimental.pallas import tpu as pltpu
from jax.sharding import PartitionSpec as P

HD = 128
HEADS = 4
EPS = 1e-06
THETA = 1000000.0
SUB = 16
PIECES = 4
BOUNDS = (0, 1024, 2048, 3072, 4096, 4608, 5120)
STRIPS = len(BOUNDS) - 1
MESH = pl.DeviceIdType.MESH
F32 = jnp.float32
BF16 = jnp.bfloat16


def dot(left, right):
    return jnp.dot(left, right, preferred_element_type=F32)


def dot_t(left, right):
    return lax.dot_general(left, right, (((1,), (1,)), ((), ())), preferred_element_type=F32)


def t_dot(left, right):
    return lax.dot_general(left, right, (((0,), (0,)), ((), ())), preferred_element_type=F32)


def stack(array):
    blocks = []
    for start in range(0, array.shape[0], SUB):
        blocks += [array[start : start + SUB, h * HD : (h + 1) * HD] for h in range(HEADS)]
    return jnp.concatenate(blocks, axis=0)


def unstack(array):
    rows = []
    for start in range(0, array.shape[0], HEADS * SUB):
        blocks = [array[start + h * SUB : start + (h + 1) * SUB] for h in range(HEADS)]
        rows.append(jnp.concatenate(blocks, axis=1))
    return jnp.concatenate(rows, axis=0)


def swap(array):
    return pltpu.roll(array, HD // 2, 1)


def tall(array):
    return jnp.concatenate([array[k] for k in range(array.shape[0]) for h in range(HEADS)], axis=0)


def ahead(compute, finish):
    finish(0, compute(0))
    waiting = compute(1)
    for p in range(2, STRIPS):
        following = compute(p)
        finish(p - 1, waiting)
        waiting = following
    finish(STRIPS - 1, waiting)


def pipe_kernel(
    sections,
    x0,
    wk_all,
    wv_all,
    wscore,
    segments,
    lengths,
    grades,
    out_key,
    out_value,
    wk,
    wv,
    wkt,
    wvt,
    slots,
    cosine,
    sine,
    mask,
    ends,
    levels,
    hin,
    gin,
    gkv,
    mixs,
    hout,
    gout,
    keys,
    values,
    probs,
    scales,
    carry_v,
    carry_k,
    peer_h,
    peer_g,
    peer_gkv,
    peer_mix,
    total,
    pair_out,
    pair_in,
    first_out,
    first_in,
    second_out,
    second_in,
    weight_sem,
    hsend,
    hrecv,
    gsend,
    grecv,
    xsend,
    xrecv,
    pair_send,
    pair_recv,
    first_send,
    first_recv,
    second_send,
    second_recv,
):
    section = lax.axis_index("section")
    place = lax.axis_index("dp")
    x, y, core = place // 8, (place // 2) % 4, place % 2
    xpeers = [((x + r) % 4) * 8 + place % 8 for r in range(1, 4)]
    sibling = x * 8 + y * 2 + (1 - core)
    beside = y + 1 - 2 * (y % 2)
    across = 3 - y
    opposite = (y + 2) % 4
    ydevices = [x * 8 + beside * 2 + core, x * 8 + across * 2 + core]
    last = sections - 1
    chunks = hin.shape[0]
    model = hin.shape[2]
    piece = model // PIECES
    up = jnp.minimum(section + 1, last)
    down = jnp.maximum(section - 1, 0)

    def columns(p):
        return pl.ds(BOUNDS[p], BOUNDS[p + 1] - BOUNDS[p])

    rows = HEADS * SUB
    def load_weight(p):
        there = columns(p)
        return [
            pltpu.make_async_copy(source.at[there], target.at[there], weight_sem.at[k, p])
            for k, source, target in ((0, wk_all, wk), (1, wv_all, wv))
        ]

    for p in range(STRIPS):
        for copy in load_weight(p):
            copy.start()

    @pl.when(section == 0)
    def _():
        def load(c, unused):
            for p in range(STRIPS):
                there = columns(p)
                pltpu.make_async_copy(
                    x0.at[c, :, there], hin.at[c, :, there], hrecv.at[c, p]
                ).start()
            return unused

        lax.fori_loop(0, chunks, load, 0)

    barrier = pltpu.get_barrier_semaphore()

    @pl.when(section < last)
    def _():
        pl.semaphore_signal(barrier, inc=1, device_id={"section": up}, device_id_type=MESH)

    @pl.when(section > 0)
    def _():
        pl.semaphore_signal(barrier, inc=1, device_id={"section": down}, device_id_type=MESH)

    for peer in xpeers + ydevices + [sibling]:
        pl.semaphore_signal(barrier, inc=1, device_id={"dp": peer}, device_id_type=MESH)

    keys[...] = jnp.zeros_like(keys)
    values[...] = jnp.zeros_like(values)
    source = lax.broadcasted_iota(jnp.int32, (slots.shape[0] * 4, 2 * rows), 0)
    lane = lax.broadcasted_iota(jnp.int32, (slots.shape[0] * 4, 2 * rows), 1)
    spread = (source == (lane // rows) * SUB + lane % SUB).astype(BF16)
    both = jnp.concatenate([segments[...], grades[...]], axis=0).astype(F32).astype(BF16)
    slots[...] = dot(both, spread)

    def make_tables(c, unused):
        row, half = c // 2, lax.rem(c, 2)
        sub = lax.broadcasted_iota(jnp.int32, (rows, 2 * rows), 0)
        lane = lax.broadcasted_iota(jnp.int32, (rows, 2 * rows), 1)
        slot_i = half * SUB + sub % SUB
        slot_j = (lane // rows) * SUB + lane % SUB
        seg_j = jnp.broadcast_to(slots[pl.ds(row, 1), :], (rows, 2 * rows))
        grade_j = jnp.broadcast_to(slots[pl.ds(row + chunks // 2, 1), :], (rows, 2 * rows))
        here = lane == half * rows + sub
        seg_i = jnp.sum(jnp.where(here, seg_j, 0.0), axis=1, keepdims=True)
        grade_i = jnp.sum(jnp.where(here, grade_j, 0.0), axis=1, keepdims=True)
        entry = lax.broadcasted_iota(jnp.int32, lengths.shape, 1)
        length = jnp.sum(
            jnp.where(entry == row, lengths[...].astype(F32), 0.0), axis=1, keepdims=True
        )
        length = jnp.broadcast_to(length, (rows, 2 * rows)).astype(jnp.int32)
        same = seg_j == seg_i
        live = slot_i < length
        allowed = (same & (slot_j <= slot_i) & live & (slot_j < length)) | (slot_i == slot_j)
        heads = sub // SUB == (lane // SUB) % HEADS
        mask[c] = jnp.where(allowed & heads, 1.0, 0.0)
        once = (lane // SUB) % HEADS == 0
        before = jnp.sum(jnp.where(once & (seg_j < seg_i), 1.0, 0.0), axis=1, keepdims=True)
        after = jnp.sum(
            jnp.where(once & same & (slot_j > slot_i), 1.0, 0.0), axis=1, keepdims=True
        )
        final = (after == 0.0) | (slot_i == length - 1)
        ends[c] = jnp.where(live & final, 1.0, 0.0)[:SUB, :1]
        levels[c] = grade_i[:SUB]
        position = slot_i[:SUB].astype(F32) - before[:SUB]
        lane = lane[:SUB]
        freqs = jnp.exp((lane % (HD // 2)).astype(F32) * (-2.0 * math.log(THETA) / HD))
        angles = position * freqs
        cosine[c] = jnp.cos(angles)
        sine[c] = jnp.where(lane < HD // 2, -1.0, 1.0) * jnp.sin(angles)
        return unused

    lax.fori_loop(0, chunks, make_tables, 0)

    @pl.when(section > 0)
    def _():
        for p in range(STRIPS):
            for copy in load_weight(p):
                copy.wait()

    @pl.when((section > 0) & (section < last))
    def _():
        pl.semaphore_wait(barrier, 8)

    @pl.when((section == 0) | (section == last))
    def _():
        pl.semaphore_wait(barrier, 7)

    def turn(source, target):
        def block(t, unused):
            there = pl.ds(pl.multiple_of(t * 256, 256), 256)
            target[:, there] = source[there, :].T
            return unused

        lax.fori_loop(0, model // 256, block, 0)

    @pl.when(section > 0)
    def _():
        turn(wv, wvt)

    @pl.when(section > 1)
    def _():
        turn(wk, wkt)

    def h_copy(c, p):
        return pltpu.make_async_remote_copy(
            src_ref=hout.at[c, :, columns(p)],
            dst_ref=hin.at[c, :, columns(p)],
            send_sem=hsend.at[c, p],
            recv_sem=hrecv.at[c, p],
            device_id={"section": up},
            device_id_type=MESH,
        )

    def g_copy(c, p):
        return pltpu.make_async_remote_copy(
            src_ref=gout.at[c, :, columns(p)],
            dst_ref=gin.at[c, :, columns(p)],
            send_sem=gsend.at[c, p],
            recv_sem=grecv.at[c, p],
            device_id={"section": down},
            device_id_type=MESH,
        )

    def x_copy(kind, c, r):
        peer = (x + r) % 4
        source, target = (
            (hin.at[c, :, pl.ds(pl.multiple_of(peer * piece, 128), piece)], peer_h),
            (mixs.at[c], peer_mix),
            (gin.at[c, :, pl.ds(pl.multiple_of(peer * piece, 128), piece)], peer_g),
            (gkv.at[c], peer_gkv),
        )[kind]
        return pltpu.make_async_remote_copy(
            src_ref=source,
            dst_ref=target.at[r - 1, c],
            send_sem=xsend.at[kind, c, r - 1],
            recv_sem=xrecv.at[kind, c, r - 1],
            device_id={"dp": xpeers[r - 1]},
            device_id_type=MESH,
        )

    def forward(c, n, origin=False):
        some = pl.ds(c, n)
        lines = n * SUB
        row = c // 2

        def held(p):
            part = hin[some, :, columns(p)]
            return part.reshape(lines, part.shape[-1])

        acc_k = jnp.zeros((lines, HEADS * HD), F32)
        acc_v = jnp.zeros((lines, HEADS * HD), F32)
        square = jnp.zeros((lines, 1), F32)
        for p in range(STRIPS):
            for k in range(n):
                h_copy(c + k, p).wait_recv()
            if origin:

                @pl.when(c == 0)
                def _():
                    for copy in load_weight(p):
                        copy.wait()

            part = held(p)
            acc_k += dot(part, wk[columns(p), :])
            acc_v += dot(part, wv[columns(p), :])
            full = part.astype(F32)
            square += jnp.sum(full * full, axis=1, keepdims=True)
        scale = lax.rsqrt(square / model + EPS)
        scales[some] = scale.reshape(n, SUB, 1)
        turned = stack(acc_k * scale)
        turned = turned * tall(cosine[some]) + swap(turned) * tall(sine[some])
        key = turned.astype(BF16)
        value = stack(acc_v * scale).astype(BF16)
        keys[some] = key.reshape(n, rows, HD)
        values[some] = value.reshape(n, rows, HD)
        all_keys = keys[pl.ds(row * 2, 2)].reshape(2 * rows, HD)
        all_values = values[pl.ds(row * 2, 2)].reshape(2 * rows, HD)
        logits = dot_t(key, all_keys) * (1.0 / HD)
        logits = jnp.where(mask[some].reshape(n * rows, 2 * rows) > 0.0, logits, -1e30)
        top = jnp.max(logits, axis=1, keepdims=True)
        expd = jnp.exp(logits - top)
        prob = expd / jnp.sum(expd, axis=1, keepdims=True)
        probs[some] = prob.reshape(n, rows, 2 * rows)
        mixed = unstack(dot(prob.astype(BF16), all_values).astype(BF16))
        mixs[some] = mixed.reshape(n, SUB, HEADS * HD)

        def strip_of(p, product):
            return (held(p).astype(F32) + product).astype(BF16).reshape(n, SUB, -1)

        def send(p, out):
            hout[some, :, columns(p)] = out
            if n == 1:
                h_copy(c, p).start()

        if origin:
            ahead(lambda p: strip_of(p, dot_t(mixed, wv[columns(p), :])), send)
        else:
            ahead(lambda p: strip_of(p, dot(mixed, wvt[:, columns(p)])), send)

        for k in range(n):
            for r in range(1, 4):
                x_copy(0, c + k, r).start()
                x_copy(1, c + k, r).start()

    def loss(c):
        some = pl.ds(c, 2)
        square = jnp.zeros((2, SUB, 1), F32)
        score = jnp.zeros((2, SUB, 1), F32)
        for p in range(STRIPS):
            full = hout[some, :, columns(p)].astype(F32)
            square += jnp.sum(full * full, axis=2, keepdims=True)
            score += jnp.sum(full * wscore[:, columns(p)][None], axis=2, keepdims=True)
        scale = lax.rsqrt(square / model + EPS)
        score = score * scale
        end = ends[some]

        def softmax(entries):
            masked = jnp.where(end > 0.0, entries, -1e30)
            top = jnp.max(jnp.max(masked, axis=0), axis=0, keepdims=True)
            expd = jnp.where(end > 0.0, jnp.exp(masked - top[None]), 0.0)
            return expd / jnp.sum(jnp.sum(expd, axis=0), axis=0, keepdims=True)[None]

        weight = jnp.where(end > 0.0, softmax(score) - softmax(levels[some]), 0.0)
        first = scale * weight
        second = scale * scale * weight * score * (1.0 / model)
        for p in range(STRIPS):
            full = hout[some, :, columns(p)].astype(F32)
            grad = first * wscore[:, columns(p)][None] - second * full
            gin[some, :, columns(p)] = grad.astype(BF16)

    def backward(c, n, origin=False):
        some = pl.ds(c, n)
        lines = n * SUB
        row = c // 2

        def grad_at(p):
            part = gin[some, :, columns(p)]
            return part.reshape(lines, part.shape[-1])

        acc = jnp.zeros((lines, HEADS * HD), F32)
        for p in range(STRIPS):
            if n == 1:
                g_copy(c, p).wait_recv()
            acc += dot(grad_at(p), wv[columns(p), :])
        scale = scales[some].reshape(lines, 1)
        grad_mixed = stack(acc).astype(BF16)
        all_keys = keys[pl.ds(row * 2, 2)].reshape(2 * rows, HD)
        all_values = values[pl.ds(row * 2, 2)].reshape(2 * rows, HD)
        key = keys[some].reshape(n * rows, HD)
        value = values[some].reshape(n * rows, HD)
        prob = probs[some].reshape(n * rows, 2 * rows)
        grad_probs = dot_t(grad_mixed, all_values)
        product = prob * grad_probs
        grad_scores = (product - prob * jnp.sum(product, axis=1, keepdims=True)).astype(BF16)
        own_v = t_dot(prob.astype(BF16), grad_mixed)
        own_k = t_dot(grad_scores, key)
        if n == 1:
            second = lax.rem(c, 2) == 1
            from_v, from_k = own_v, own_k
            own_v = jnp.where(second, from_v[rows:], from_v[:rows] + carry_v[...])
            own_k = jnp.where(second, from_k[rows:], from_k[:rows] + carry_k[...])
            carry_v[...] = from_v[:rows]
            carry_k[...] = from_k[:rows]
        turned = (dot(grad_scores, all_keys) + own_k) * (1.0 / HD)
        along = jnp.sum(turned * key.astype(F32) + own_v * value.astype(F32), axis=1, keepdims=True)
        along = jnp.sum(along.reshape(n, HEADS, SUB, 1), axis=1).reshape(lines, 1)
        along = along * (scale * scale) * (1.0 / model)
        grad_key = turned * tall(cosine[some]) - swap(turned) * tall(sine[some])
        flat_key = unstack(grad_key.astype(BF16))
        flat_value = unstack(own_v.astype(BF16))
        if not origin:

            def strip_of(p):
                grad = dot(flat_key, wkt[:, columns(p)]) + dot(flat_value, wvt[:, columns(p)])
                full = hin[some, :, columns(p)].reshape(lines, -1).astype(F32)
                out = grad_at(p).astype(F32) + scale * grad - along * full
                return out.astype(BF16).reshape(n, SUB, -1)

            def send(p, out):
                gout[some, :, columns(p)] = out
                g_copy(c + n - 1, p).start()

            ahead(strip_of, send)
            if n == 2:
                for p in range(STRIPS):
                    g_copy(c, p).start()

        features = HEADS * HD
        key_part = (flat_key.astype(F32) * scale).astype(BF16)
        value_part = (flat_value.astype(F32) * scale).astype(BF16)
        gkv[some, :, :features] = key_part.reshape(n, SUB, features)
        gkv[some, :, features:] = value_part.reshape(n, SUB, features)

        for k in range(n):
            for r in range(1, 4):
                x_copy(2, c + k, r).start()
                x_copy(3, c + k, r).start()

    tile = 256
    group = chunks // 2

    share = piece // 8
    half_features = HEADS * HD
    sides = [pl.ds(0, half_features), pl.ds(half_features, half_features)]

    def rows_of(ypart, corepart):
        return pl.ds(pl.multiple_of((ypart * 2 + corepart) * share, 32), share)

    def pair_copy(k):
        return pltpu.make_async_remote_copy(
            src_ref=pair_out.at[k],
            dst_ref=pair_in.at[k],
            send_sem=pair_send.at[k],
            recv_sem=pair_recv.at[k],
            device_id={"dp": sibling},
            device_id_type=MESH,
        )

    def weights(base):
        def arrive(c, unused):
            for kind in range(4):
                for r in range(1, 4):
                    x_copy(kind, base + c, r).wait_recv()
            return unused

        lax.fori_loop(0, group, arrive, 0)
        which = pl.ds(base, group)

        def gather(own, peers):
            own = own.reshape(group * SUB, own.shape[-1])
            peers = peers.reshape(3 * group * SUB, peers.shape[-1])
            return jnp.concatenate([own, peers], axis=0)

        def block(t, unused):
            there = pl.ds(pl.multiple_of(t * tile, tile), tile)
            mine = pl.ds(pl.multiple_of(x * piece + t * tile, 128), tile)
            hidden = gather(hin[which, :, mine], peer_h[:, which, :, there])
            grads = gather(gin[which, :, mine], peer_g[:, which, :, there])
            both = gather(gkv[which], peer_gkv[:, which])
            mixed = gather(mixs[which], peer_mix[:, which])
            features = HEADS * HD
            part_key = t_dot(hidden, both[:, :features])
            part_value = t_dot(hidden, both[:, features:]) + t_dot(grads, mixed)

            @pl.when(base == 0)
            def _():
                total[there, :features] = part_key
                total[there, features:] = part_value

            @pl.when(base > 0)
            def _():
                total[there, :features] = part_key + total[there, :features]
                total[there, features:] = part_value + total[there, features:]

            for k in range(4):
                ready = ((k * 2 + 2 - core) * share + tile - 1) // tile - 1

                @pl.when((base > 0) & (t == ready))
                def _():
                    pair_out[k] = total[rows_of(k, 1 - core), :].astype(BF16)
                    pair_copy(k).start()

            return unused

        lax.fori_loop(0, piece // tile, block, 0)

    def first_copy(side, k):
        return pltpu.make_async_remote_copy(
            src_ref=first_out.at[side, k],
            dst_ref=first_in.at[side, k],
            send_sem=first_send.at[side, k],
            recv_sem=first_recv.at[side, k],
            device_id={"dp": ydevices[side]},
            device_id_type=MESH,
        )

    def second_copy(side):
        return pltpu.make_async_remote_copy(
            src_ref=second_out.at[side],
            dst_ref=second_in.at[side],
            send_sem=second_send.at[side],
            recv_sem=second_recv.at[side],
            device_id={"dp": ydevices[1 - side]},
            device_id_type=MESH,
        )

    def scatter():
        order = [opposite, beside, across, y]
        for k in range(4):
            pair_copy(k).wait_recv()

        def held(k, side):
            other = pair_in[order[k], :, sides[side]].astype(F32)
            return total[rows_of(order[k], core), sides[side]] + other

        for side in range(2):
            first_out[side, 1] = held(0, side).astype(BF16)
            first_copy(side, 1).start()
        for side in range(2):
            first_out[side, 0] = held(1 + side, side).astype(BF16)
            first_copy(side, 0).start()
        for side in range(2):
            first_copy(side, 1).wait_recv()
            second_out[side] = (held(2 - side, side) + first_in[side, 1].astype(F32)).astype(BF16)
            second_copy(side).start()
        for side, out in ((0, out_key), (1, out_value)):
            first_copy(side, 0).wait_recv()
            second_copy(side).wait_recv()
            out[...] = held(3, side) + first_in[side, 0].astype(F32) + second_in[side].astype(F32)
        for k in range(4):
            pair_copy(k).wait_send()
        for side in range(2):
            first_copy(side, 0).wait_send()
            first_copy(side, 1).wait_send()
            second_copy(side).wait_send()

    lead = jnp.where(section == last - 1, 5, chunks)

    def slot(i, unused):
        @pl.when((i < chunks) & (section == 0))
        def _():
            forward(i, 1, True)

        @pl.when((i < chunks) & (section > 0))
        def _():
            forward(i, 1)

        j = i - lead

        @pl.when((j == 0) & (section == 1))
        def _():
            turn(wk, wkt)

        c = (j // 2) * 2 + 1 - lax.rem(j, 2)

        @pl.when((j >= 0) & (j < chunks) & (section == 0))
        def _():
            backward(c, 1, True)

        @pl.when((j >= 0) & (j < chunks) & (section > 0))
        def _():
            backward(c, 1)

        @pl.when((j == group + 1) & (section == 0))
        def _():
            weights(0)

        return unused

    def whole(row, unused):
        forward(row * 2, 2)
        loss(row * 2)
        backward(row * 2, 2)
        return unused

    @pl.when(section < last)
    def _():
        lax.fori_loop(0, 2 * chunks, slot, 0)

    @pl.when(section == last)
    def _():
        lax.fori_loop(0, chunks // 2, whole, 0)

    def rest(step, unused):
        weights(step * group)
        return unused

    lax.fori_loop(jnp.where(section == 0, 1, 0), 2, rest, 0)
    scatter()

    def drain(c, unused):
        for p in range(STRIPS):

            @pl.when(section < last)
            def _():
                h_copy(c, p).wait_send()

            @pl.when(section > 0)
            def _():
                g_copy(c, p).wait_send()

        for kind in range(4):
            for r in range(1, 4):
                x_copy(kind, c, r).wait_send()
        return unused

    lax.fori_loop(0, chunks, drain, 0)


def finish_kernel(key_in, value_in, key_out, value_out):
    key_out[0] = key_in[...]
    value_out[0] = value_in[...]


def shards(x0, w_key, w_value, w_score, segments, lengths, grades):
    sections = lax.axis_size("section")
    micro, width, model = x0.shape
    features = w_key.shape[2]
    chunks = micro * width // SUB
    vmem = pl.BlockSpec(memory_space=pltpu.VMEM)
    act = (chunks, SUB, model)
    flat = (chunks, SUB, features)
    stacked = (chunks, HEADS * SUB, HD)
    piece = model // PIECES
    share = piece // 8
    dma = pltpu.SemaphoreType.DMA
    grad_key, grad_value = pl.pallas_call(
        functools.partial(pipe_kernel, sections),
        out_shape=[jax.ShapeDtypeStruct((share, features), F32)] * 2,
        in_specs=[pl.BlockSpec(memory_space=pl.ANY)] * 3 + [vmem] * 4,
        out_specs=[vmem] * 2,
        scratch_shapes=[
            pltpu.VMEM((model, features), BF16),
            pltpu.VMEM((model, features), BF16),
            pltpu.VMEM((features, model), BF16),
            pltpu.VMEM((features, model), BF16),
            pltpu.VMEM((2 * micro, HD), F32),
            pltpu.VMEM((chunks, SUB, HD), F32),
            pltpu.VMEM((chunks, SUB, HD), F32),
            pltpu.VMEM((chunks, HEADS * SUB, 2 * HEADS * SUB), F32),
            pltpu.VMEM((chunks, SUB, 1), F32),
            pltpu.VMEM((chunks, SUB, 1), F32),
            pltpu.VMEM(act, BF16),
            pltpu.VMEM(act, BF16),
            pltpu.VMEM((chunks, SUB, 2 * features), BF16),
            pltpu.VMEM(flat, BF16),
            pltpu.VMEM(act, BF16),
            pltpu.VMEM(act, BF16),
            pltpu.VMEM(stacked, BF16),
            pltpu.VMEM(stacked, BF16),
            pltpu.VMEM((chunks, HEADS * SUB, 2 * HEADS * SUB), F32),
            pltpu.VMEM((chunks, SUB, 1), F32),
            pltpu.VMEM((HEADS * SUB, HD), F32),
            pltpu.VMEM((HEADS * SUB, HD), F32),
            pltpu.VMEM((3, chunks, SUB, piece), BF16),
            pltpu.VMEM((3, chunks, SUB, piece), BF16),
            pltpu.VMEM((3, chunks, SUB, 2 * features), BF16),
            pltpu.VMEM((3, chunks, SUB, features), BF16),
            pltpu.VMEM((piece, 2 * features), F32),
            pltpu.VMEM((4, share, 2 * features), BF16),
            pltpu.VMEM((4, share, 2 * features), BF16),
            pltpu.VMEM((2, 2, share, features), BF16),
            pltpu.VMEM((2, 2, share, features), BF16),
            pltpu.VMEM((2, share, features), BF16),
            pltpu.VMEM((2, share, features), BF16),
            dma((2, STRIPS)),
            dma((chunks, STRIPS)),
            dma((chunks, STRIPS)),
            dma((chunks, STRIPS)),
            dma((chunks, STRIPS)),
            dma((4, chunks, 3)),
            dma((4, chunks, 3)),
            dma((4,)),
            dma((4,)),
            dma((2, 2)),
            dma((2, 2)),
            dma((2,)),
            dma((2,)),
        ],
        compiler_params=pltpu.CompilerParams(
            collective_id=0, has_side_effects=True, vmem_limit_bytes=56 * 2**20
        ),
    )(
        x0.reshape(act),
        w_key[0],
        w_value[0],
        w_score.reshape(1, model),
        segments,
        lengths.reshape(1, micro),
        grades,
    )
    grad_key, grad_value = pl.pallas_call(
        finish_kernel,
        out_shape=[jax.ShapeDtypeStruct((1, share, features), F32)] * 2,
        in_specs=[vmem] * 2,
        out_specs=[vmem] * 2,
    )(grad_key, grad_value)
    return (grad_key, grad_value)


def solution(mesh):
    placed = (
        P(None, "dp", None),
        P("section", None, None),
        P("section", None, None),
        P(),
        P(None, "dp"),
        P(None, "dp"),
        P(None, "dp"),
    )
    return jax.shard_map(
        shards,
        mesh=mesh,
        in_specs=placed,
        out_specs=(P("section", "dp", None), P("section", "dp", None)),
        check_vma=False,
    )
```

```python
import functools
import math

import jax
import jax.numpy as jnp
from jax import lax
from jax.experimental import pallas as pl
from jax.experimental.pallas import tpu as pltpu
from jax.sharding import PartitionSpec as P

HD = 128
HEADS = 4
EPS = 1e-06
THETA = 1000000.0
SUB = 16
PIECES = 4
BOUNDS = (0, 1024, 2048, 3072, 4096, 4608, 5120)
STRIPS = len(BOUNDS) - 1
MESH = pl.DeviceIdType.MESH
F32 = jnp.float32
BF16 = jnp.bfloat16


def dot(left, right):
    return jnp.dot(left, right, preferred_element_type=F32)


def dot_t(left, right):
    return lax.dot_general(left, right, (((1,), (1,)), ((), ())), preferred_element_type=F32)


def t_dot(left, right):
    return lax.dot_general(left, right, (((0,), (0,)), ((), ())), preferred_element_type=F32)


def stack(array):
    blocks = []
    for start in range(0, array.shape[0], SUB):
        blocks += [array[start : start + SUB, h * HD : (h + 1) * HD] for h in range(HEADS)]
    return jnp.concatenate(blocks, axis=0)


def unstack(array):
    rows = []
    for start in range(0, array.shape[0], HEADS * SUB):
        blocks = [array[start + h * SUB : start + (h + 1) * SUB] for h in range(HEADS)]
        rows.append(jnp.concatenate(blocks, axis=1))
    return jnp.concatenate(rows, axis=0)


def swap(array):
    return pltpu.roll(array, HD // 2, 1)


def tall(array):
    return jnp.concatenate([array[k] for k in range(array.shape[0]) for h in range(HEADS)], axis=0)


def ahead(compute, finish):
    finish(0, compute(0))
    waiting = compute(1)
    for p in range(2, STRIPS):
        following = compute(p)
        finish(p - 1, waiting)
        waiting = following
    finish(STRIPS - 1, waiting)


def pipe_kernel(
    sections,
    x0,
    wk_all,
    wv_all,
    wscore,
    segments,
    lengths,
    grades,
    out_key,
    out_value,
    wk,
    wv,
    wkt,
    wvt,
    slots,
    cosine,
    sine,
    mask,
    ends,
    levels,
    hin,
    gin,
    gkv,
    mixs,
    hout,
    gout,
    keys,
    values,
    probs,
    scales,
    carry_v,
    carry_k,
    peer_h,
    peer_g,
    peer_gkv,
    peer_mix,
    total,
    pair_out,
    pair_in,
    first_out,
    first_in,
    second_out,
    second_in,
    weight_sem,
    hsend,
    hrecv,
    gsend,
    grecv,
    xsend,
    xrecv,
    pair_send,
    pair_recv,
    first_send,
    first_recv,
    second_send,
    second_recv,
):
    section = lax.axis_index("section")
    place = lax.axis_index("dp")
    x, y, core = place // 8, (place // 2) % 4, place % 2
    xpeers = [((x + r) % 4) * 8 + place % 8 for r in range(1, 4)]
    sibling = x * 8 + y * 2 + (1 - core)
    beside = y + 1 - 2 * (y % 2)
    across = 3 - y
    opposite = (y + 2) % 4
    ydevices = [x * 8 + beside * 2 + core, x * 8 + across * 2 + core]
    last = sections - 1
    chunks = hin.shape[0]
    model = hin.shape[2]
    piece = model // PIECES
    up = jnp.minimum(section + 1, last)
    down = jnp.maximum(section - 1, 0)

    def columns(p):
        return pl.ds(BOUNDS[p], BOUNDS[p + 1] - BOUNDS[p])

    rows = HEADS * SUB
    def load_weight(p):
        there = columns(p)
        return [
            pltpu.make_async_copy(source.at[there], target.at[there], weight_sem.at[k, p])
            for k, source, target in ((0, wk_all, wk), (1, wv_all, wv))
        ]

    for p in range(STRIPS):
        for copy in load_weight(p):
            copy.start()

    @pl.when(section == 0)
    def _():
        def load(c, unused):
            for p in range(STRIPS):
                there = columns(p)
                pltpu.make_async_copy(
                    x0.at[c, :, there], hin.at[c, :, there], hrecv.at[c, p]
                ).start()
            return unused

        lax.fori_loop(0, chunks, load, 0)

    barrier = pltpu.get_barrier_semaphore()

    @pl.when(section < last)
    def _():
        pl.semaphore_signal(barrier, inc=1, device_id={"section": up}, device_id_type=MESH)

    @pl.when(section > 0)
    def _():
        pl.semaphore_signal(barrier, inc=1, device_id={"section": down}, device_id_type=MESH)

    for peer in xpeers + ydevices + [sibling]:
        pl.semaphore_signal(barrier, inc=1, device_id={"dp": peer}, device_id_type=MESH)

    keys[...] = jnp.zeros_like(keys)
    values[...] = jnp.zeros_like(values)
    source = lax.broadcasted_iota(jnp.int32, (slots.shape[0] * 4, 2 * rows), 0)
    lane = lax.broadcasted_iota(jnp.int32, (slots.shape[0] * 4, 2 * rows), 1)
    spread = (source == (lane // rows) * SUB + lane % SUB).astype(BF16)
    both = jnp.concatenate([segments[...], grades[...]], axis=0).astype(F32).astype(BF16)
    slots[...] = dot(both, spread)

    def make_tables(c, unused):
        row, half = c // 2, lax.rem(c, 2)
        sub = lax.broadcasted_iota(jnp.int32, (rows, 2 * rows), 0)
        lane = lax.broadcasted_iota(jnp.int32, (rows, 2 * rows), 1)
        slot_i = half * SUB + sub % SUB
        slot_j = (lane // rows) * SUB + lane % SUB
        seg_j = jnp.broadcast_to(slots[pl.ds(row, 1), :], (rows, 2 * rows))
        grade_j = jnp.broadcast_to(slots[pl.ds(row + chunks // 2, 1), :], (rows, 2 * rows))
        here = lane == half * rows + sub
        seg_i = jnp.sum(jnp.where(here, seg_j, 0.0), axis=1, keepdims=True)
        grade_i = jnp.sum(jnp.where(here, grade_j, 0.0), axis=1, keepdims=True)
        entry = lax.broadcasted_iota(jnp.int32, lengths.shape, 1)
        length = jnp.sum(
            jnp.where(entry == row, lengths[...].astype(F32), 0.0), axis=1, keepdims=True
        )
        length = jnp.broadcast_to(length, (rows, 2 * rows)).astype(jnp.int32)
        same = seg_j == seg_i
        live = slot_i < length
        allowed = (same & (slot_j <= slot_i) & live & (slot_j < length)) | (slot_i == slot_j)
        heads = sub // SUB == (lane // SUB) % HEADS
        mask[c] = jnp.where(allowed & heads, 1.0, 0.0)
        once = (lane // SUB) % HEADS == 0
        before = jnp.sum(jnp.where(once & (seg_j < seg_i), 1.0, 0.0), axis=1, keepdims=True)
        after = jnp.sum(
            jnp.where(once & same & (slot_j > slot_i), 1.0, 0.0), axis=1, keepdims=True
        )
        final = (after == 0.0) | (slot_i == length - 1)
        ends[c] = jnp.where(live & final, 1.0, 0.0)[:SUB, :1]
        levels[c] = grade_i[:SUB]
        position = slot_i[:SUB].astype(F32) - before[:SUB]
        lane = lane[:SUB]
        freqs = jnp.exp((lane % (HD // 2)).astype(F32) * (-2.0 * math.log(THETA) / HD))
        angles = position * freqs
        cosine[c] = jnp.cos(angles)
        sine[c] = jnp.where(lane < HD // 2, -1.0, 1.0) * jnp.sin(angles)
        return unused

    lax.fori_loop(0, chunks, make_tables, 0)

    @pl.when(section > 0)
    def _():
        for p in range(STRIPS):
            for copy in load_weight(p):
                copy.wait()

    @pl.when((section > 0) & (section < last))
    def _():
        pl.semaphore_wait(barrier, 8)

    @pl.when((section == 0) | (section == last))
    def _():
        pl.semaphore_wait(barrier, 7)

    def turn(source, target):
        def block(t, unused):
            there = pl.ds(pl.multiple_of(t * 256, 256), 256)
            target[:, there] = source[there, :].T
            return unused

        lax.fori_loop(0, model // 256, block, 0)

    @pl.when(section > 0)
    def _():
        turn(wv, wvt)

    @pl.when(section > 1)
    def _():
        turn(wk, wkt)

    def h_copy(c, p):
        return pltpu.make_async_remote_copy(
            src_ref=hout.at[c, :, columns(p)],
            dst_ref=hin.at[c, :, columns(p)],
            send_sem=hsend.at[c, p],
            recv_sem=hrecv.at[c, p],
            device_id={"section": up},
            device_id_type=MESH,
        )

    def g_copy(c, p):
        return pltpu.make_async_remote_copy(
            src_ref=gout.at[c, :, columns(p)],
            dst_ref=gin.at[c, :, columns(p)],
            send_sem=gsend.at[c, p],
            recv_sem=grecv.at[c, p],
            device_id={"section": down},
            device_id_type=MESH,
        )

    def x_copy(kind, c, r):
        peer = (x + r) % 4
        source, target = (
            (hin.at[c, :, pl.ds(pl.multiple_of(peer * piece, 128), piece)], peer_h),
            (mixs.at[c], peer_mix),
            (gin.at[c, :, pl.ds(pl.multiple_of(peer * piece, 128), piece)], peer_g),
            (gkv.at[c], peer_gkv),
        )[kind]
        return pltpu.make_async_remote_copy(
            src_ref=source,
            dst_ref=target.at[r - 1, c],
            send_sem=xsend.at[kind, c, r - 1],
            recv_sem=xrecv.at[kind, c, r - 1],
            device_id={"dp": xpeers[r - 1]},
            device_id_type=MESH,
        )

    def forward(c, n, origin=False):
        some = pl.ds(c, n)
        lines = n * SUB
        row = c // 2

        def held(p):
            part = hin[some, :, columns(p)]
            return part.reshape(lines, part.shape[-1])

        acc_k = jnp.zeros((lines, HEADS * HD), F32)
        acc_v = jnp.zeros((lines, HEADS * HD), F32)
        square = jnp.zeros((lines, 1), F32)
        for p in range(STRIPS):
            for k in range(n):
                h_copy(c + k, p).wait_recv()
            if origin:

                @pl.when(c == 0)
                def _():
                    for copy in load_weight(p):
                        copy.wait()

            part = held(p)
            acc_k += dot(part, wk[columns(p), :])
            acc_v += dot(part, wv[columns(p), :])
            full = part.astype(F32)
            square += jnp.sum(full * full, axis=1, keepdims=True)
        scale = lax.rsqrt(square / model + EPS)
        scales[some] = scale.reshape(n, SUB, 1)
        turned = stack(acc_k * scale)
        turned = turned * tall(cosine[some]) + swap(turned) * tall(sine[some])
        key = turned.astype(BF16)
        value = stack(acc_v * scale).astype(BF16)
        keys[some] = key.reshape(n, rows, HD)
        values[some] = value.reshape(n, rows, HD)
        all_keys = keys[pl.ds(row * 2, 2)].reshape(2 * rows, HD)
        all_values = values[pl.ds(row * 2, 2)].reshape(2 * rows, HD)
        logits = dot_t(key, all_keys) * (1.0 / HD)
        logits = jnp.where(mask[some].reshape(n * rows, 2 * rows) > 0.0, logits, -1e30)
        top = jnp.max(logits, axis=1, keepdims=True)
        expd = jnp.exp(logits - top)
        prob = expd / jnp.sum(expd, axis=1, keepdims=True)
        probs[some] = prob.reshape(n, rows, 2 * rows)
        mixed = unstack(dot(prob.astype(BF16), all_values).astype(BF16))
        mixs[some] = mixed.reshape(n, SUB, HEADS * HD)

        def strip_of(p, product):
            return (held(p).astype(F32) + product).astype(BF16).reshape(n, SUB, -1)

        def send(p, out):
            hout[some, :, columns(p)] = out
            if n == 1:
                h_copy(c, p).start()

        if origin:
            ahead(lambda p: strip_of(p, dot_t(mixed, wv[columns(p), :])), send)
        else:
            ahead(lambda p: strip_of(p, dot(mixed, wvt[:, columns(p)])), send)

        for k in range(n):
            for r in (2, 1, 3):
                x_copy(0, c + k, r).start()
                x_copy(1, c + k, r).start()

    def loss(c):
        some = pl.ds(c, 2)
        square = jnp.zeros((2, SUB, 1), F32)
        score = jnp.zeros((2, SUB, 1), F32)
        for p in range(STRIPS):
            full = hout[some, :, columns(p)].astype(F32)
            square += jnp.sum(full * full, axis=2, keepdims=True)
            score += jnp.sum(full * wscore[:, columns(p)][None], axis=2, keepdims=True)
        scale = lax.rsqrt(square / model + EPS)
        score = score * scale
        end = ends[some]

        def softmax(entries):
            masked = jnp.where(end > 0.0, entries, -1e30)
            top = jnp.max(jnp.max(masked, axis=0), axis=0, keepdims=True)
            expd = jnp.where(end > 0.0, jnp.exp(masked - top[None]), 0.0)
            return expd / jnp.sum(jnp.sum(expd, axis=0), axis=0, keepdims=True)[None]

        weight = jnp.where(end > 0.0, softmax(score) - softmax(levels[some]), 0.0)
        first = scale * weight
        second = scale * scale * weight * score * (1.0 / model)
        for p in range(STRIPS):
            full = hout[some, :, columns(p)].astype(F32)
            grad = first * wscore[:, columns(p)][None] - second * full
            gin[some, :, columns(p)] = grad.astype(BF16)

    def backward(c, n, origin=False):
        some = pl.ds(c, n)
        lines = n * SUB
        row = c // 2

        def grad_at(p):
            part = gin[some, :, columns(p)]
            return part.reshape(lines, part.shape[-1])

        acc = jnp.zeros((lines, HEADS * HD), F32)
        for p in range(STRIPS):
            if n == 1:
                g_copy(c, p).wait_recv()
            acc += dot(grad_at(p), wv[columns(p), :])
        scale = scales[some].reshape(lines, 1)
        grad_mixed = stack(acc).astype(BF16)
        all_keys = keys[pl.ds(row * 2, 2)].reshape(2 * rows, HD)
        all_values = values[pl.ds(row * 2, 2)].reshape(2 * rows, HD)
        key = keys[some].reshape(n * rows, HD)
        value = values[some].reshape(n * rows, HD)
        prob = probs[some].reshape(n * rows, 2 * rows)
        grad_probs = dot_t(grad_mixed, all_values)
        product = prob * grad_probs
        grad_scores = (product - prob * jnp.sum(product, axis=1, keepdims=True)).astype(BF16)
        own_v = t_dot(prob.astype(BF16), grad_mixed)
        own_k = t_dot(grad_scores, key)
        if n == 1:
            second = lax.rem(c, 2) == 1
            from_v, from_k = own_v, own_k
            own_v = jnp.where(second, from_v[rows:], from_v[:rows] + carry_v[...])
            own_k = jnp.where(second, from_k[rows:], from_k[:rows] + carry_k[...])
            carry_v[...] = from_v[:rows]
            carry_k[...] = from_k[:rows]
        turned = (dot(grad_scores, all_keys) + own_k) * (1.0 / HD)
        along = jnp.sum(turned * key.astype(F32) + own_v * value.astype(F32), axis=1, keepdims=True)
        along = jnp.sum(along.reshape(n, HEADS, SUB, 1), axis=1).reshape(lines, 1)
        along = along * (scale * scale) * (1.0 / model)
        grad_key = turned * tall(cosine[some]) - swap(turned) * tall(sine[some])
        flat_key = unstack(grad_key.astype(BF16))
        flat_value = unstack(own_v.astype(BF16))
        if not origin:

            def strip_of(p):
                grad = dot(flat_key, wkt[:, columns(p)]) + dot(flat_value, wvt[:, columns(p)])
                full = hin[some, :, columns(p)].reshape(lines, -1).astype(F32)
                out = grad_at(p).astype(F32) + scale * grad - along * full
                return out.astype(BF16).reshape(n, SUB, -1)

            def send(p, out):
                gout[some, :, columns(p)] = out
                g_copy(c + n - 1, p).start()

            ahead(strip_of, send)
            if n == 2:
                for p in range(STRIPS):
                    g_copy(c, p).start()

        features = HEADS * HD
        key_part = (flat_key.astype(F32) * scale).astype(BF16)
        value_part = (flat_value.astype(F32) * scale).astype(BF16)
        gkv[some, :, :features] = key_part.reshape(n, SUB, features)
        gkv[some, :, features:] = value_part.reshape(n, SUB, features)

        for k in range(n):
            for r in (2, 1, 3):
                x_copy(2, c + k, r).start()
                x_copy(3, c + k, r).start()

    tile = 256
    group = chunks // 2

    share = piece // 8
    half_features = HEADS * HD
    sides = [pl.ds(0, half_features), pl.ds(half_features, half_features)]

    def rows_of(ypart, corepart):
        return pl.ds(pl.multiple_of((ypart * 2 + corepart) * share, 32), share)

    def pair_copy(k):
        return pltpu.make_async_remote_copy(
            src_ref=pair_out.at[k],
            dst_ref=pair_in.at[k],
            send_sem=pair_send.at[k],
            recv_sem=pair_recv.at[k],
            device_id={"dp": sibling},
            device_id_type=MESH,
        )

    def weights(base):
        def arrive(c, unused):
            for kind in range(4):
                for r in range(1, 4):
                    x_copy(kind, base + c, r).wait_recv()
            return unused

        lax.fori_loop(0, group, arrive, 0)
        which = pl.ds(base, group)

        def gather(own, peers):
            own = own.reshape(group * SUB, own.shape[-1])
            peers = peers.reshape(3 * group * SUB, peers.shape[-1])
            return jnp.concatenate([own, peers], axis=0)

        def block(t, unused):
            there = pl.ds(pl.multiple_of(t * tile, tile), tile)
            mine = pl.ds(pl.multiple_of(x * piece + t * tile, 128), tile)
            hidden = gather(hin[which, :, mine], peer_h[:, which, :, there])
            grads = gather(gin[which, :, mine], peer_g[:, which, :, there])
            both = gather(gkv[which], peer_gkv[:, which])
            mixed = gather(mixs[which], peer_mix[:, which])
            features = HEADS * HD
            part_key = t_dot(hidden, both[:, :features])
            part_value = t_dot(hidden, both[:, features:]) + t_dot(grads, mixed)

            @pl.when(base == 0)
            def _():
                total[there, :features] = part_key
                total[there, features:] = part_value

            @pl.when(base > 0)
            def _():
                total[there, :features] = part_key + total[there, :features]
                total[there, features:] = part_value + total[there, features:]

            for k in range(4):
                ready = ((k * 2 + 2 - core) * share + tile - 1) // tile - 1

                @pl.when((base > 0) & (t == ready))
                def _():
                    pair_out[k] = total[rows_of(k, 1 - core), :].astype(BF16)
                    pair_copy(k).start()

            return unused

        lax.fori_loop(0, piece // tile, block, 0)

    def first_copy(side, k):
        return pltpu.make_async_remote_copy(
            src_ref=first_out.at[side, k],
            dst_ref=first_in.at[side, k],
            send_sem=first_send.at[side, k],
            recv_sem=first_recv.at[side, k],
            device_id={"dp": ydevices[side]},
            device_id_type=MESH,
        )

    def second_copy(side):
        return pltpu.make_async_remote_copy(
            src_ref=second_out.at[side],
            dst_ref=second_in.at[side],
            send_sem=second_send.at[side],
            recv_sem=second_recv.at[side],
            device_id={"dp": ydevices[1 - side]},
            device_id_type=MESH,
        )

    def scatter():
        order = [opposite, beside, across, y]
        for k in range(4):
            pair_copy(k).wait_recv()

        def held(k, side):
            other = pair_in[order[k], :, sides[side]].astype(F32)
            return total[rows_of(order[k], core), sides[side]] + other

        for side in range(2):
            first_out[side, 1] = held(0, side).astype(BF16)
            first_copy(side, 1).start()
        for side in range(2):
            first_out[side, 0] = held(1 + side, side).astype(BF16)
            first_copy(side, 0).start()
        for side in range(2):
            first_copy(side, 1).wait_recv()
            second_out[side] = (held(2 - side, side) + first_in[side, 1].astype(F32)).astype(BF16)
            second_copy(side).start()
        for side, out in ((0, out_key), (1, out_value)):
            first_copy(side, 0).wait_recv()
            second_copy(side).wait_recv()
            out[...] = held(3, side) + first_in[side, 0].astype(F32) + second_in[side].astype(F32)
        for k in range(4):
            pair_copy(k).wait_send()
        for side in range(2):
            first_copy(side, 0).wait_send()
            first_copy(side, 1).wait_send()
            second_copy(side).wait_send()

    lead = jnp.where(section == last - 1, 5, chunks)

    def slot(i, unused):
        @pl.when((i < chunks) & (section == 0))
        def _():
            forward(i, 1, True)

        @pl.when((i < chunks) & (section > 0))
        def _():
            forward(i, 1)

        j = i - lead

        @pl.when((j == 0) & (section == 1))
        def _():
            turn(wk, wkt)

        c = (j // 2) * 2 + 1 - lax.rem(j, 2)

        @pl.when((j >= 0) & (j < chunks) & (section == 0))
        def _():
            backward(c, 1, True)

        @pl.when((j >= 0) & (j < chunks) & (section > 0))
        def _():
            backward(c, 1)

        @pl.when((j == group + 1) & (section == 0))
        def _():
            weights(0)

        return unused

    def whole(row, unused):
        forward(row * 2, 2)
        loss(row * 2)
        backward(row * 2, 2)
        return unused

    @pl.when(section < last)
    def _():
        lax.fori_loop(0, 2 * chunks, slot, 0)

    @pl.when(section == last)
    def _():
        lax.fori_loop(0, chunks // 2, whole, 0)

    def rest(step, unused):
        weights(step * group)
        return unused

    lax.fori_loop(jnp.where(section == 0, 1, 0), 2, rest, 0)
    scatter()

    def drain(c, unused):
        for p in range(STRIPS):

            @pl.when(section < last)
            def _():
                h_copy(c, p).wait_send()

            @pl.when(section > 0)
            def _():
                g_copy(c, p).wait_send()

        for kind in range(4):
            for r in range(1, 4):
                x_copy(kind, c, r).wait_send()
        return unused

    lax.fori_loop(0, chunks, drain, 0)


def finish_kernel(key_in, value_in, key_out, value_out):
    key_out[0] = key_in[...]
    value_out[0] = value_in[...]


def shards(x0, w_key, w_value, w_score, segments, lengths, grades):
    sections = lax.axis_size("section")
    micro, width, model = x0.shape
    features = w_key.shape[2]
    chunks = micro * width // SUB
    vmem = pl.BlockSpec(memory_space=pltpu.VMEM)
    act = (chunks, SUB, model)
    flat = (chunks, SUB, features)
    stacked = (chunks, HEADS * SUB, HD)
    piece = model // PIECES
    share = piece // 8
    dma = pltpu.SemaphoreType.DMA
    grad_key, grad_value = pl.pallas_call(
        functools.partial(pipe_kernel, sections),
        out_shape=[jax.ShapeDtypeStruct((share, features), F32)] * 2,
        in_specs=[pl.BlockSpec(memory_space=pl.ANY)] * 3 + [vmem] * 4,
        out_specs=[vmem] * 2,
        scratch_shapes=[
            pltpu.VMEM((model, features), BF16),
            pltpu.VMEM((model, features), BF16),
            pltpu.VMEM((features, model), BF16),
            pltpu.VMEM((features, model), BF16),
            pltpu.VMEM((2 * micro, HD), F32),
            pltpu.VMEM((chunks, SUB, HD), F32),
            pltpu.VMEM((chunks, SUB, HD), F32),
            pltpu.VMEM((chunks, HEADS * SUB, 2 * HEADS * SUB), F32),
            pltpu.VMEM((chunks, SUB, 1), F32),
            pltpu.VMEM((chunks, SUB, 1), F32),
            pltpu.VMEM(act, BF16),
            pltpu.VMEM(act, BF16),
            pltpu.VMEM((chunks, SUB, 2 * features), BF16),
            pltpu.VMEM(flat, BF16),
            pltpu.VMEM(act, BF16),
            pltpu.VMEM(act, BF16),
            pltpu.VMEM(stacked, BF16),
            pltpu.VMEM(stacked, BF16),
            pltpu.VMEM((chunks, HEADS * SUB, 2 * HEADS * SUB), F32),
            pltpu.VMEM((chunks, SUB, 1), F32),
            pltpu.VMEM((HEADS * SUB, HD), F32),
            pltpu.VMEM((HEADS * SUB, HD), F32),
            pltpu.VMEM((3, chunks, SUB, piece), BF16),
            pltpu.VMEM((3, chunks, SUB, piece), BF16),
            pltpu.VMEM((3, chunks, SUB, 2 * features), BF16),
            pltpu.VMEM((3, chunks, SUB, features), BF16),
            pltpu.VMEM((piece, 2 * features), F32),
            pltpu.VMEM((4, share, 2 * features), BF16),
            pltpu.VMEM((4, share, 2 * features), BF16),
            pltpu.VMEM((2, 2, share, features), BF16),
            pltpu.VMEM((2, 2, share, features), BF16),
            pltpu.VMEM((2, share, features), BF16),
            pltpu.VMEM((2, share, features), BF16),
            dma((2, STRIPS)),
            dma((chunks, STRIPS)),
            dma((chunks, STRIPS)),
            dma((chunks, STRIPS)),
            dma((chunks, STRIPS)),
            dma((4, chunks, 3)),
            dma((4, chunks, 3)),
            dma((4,)),
            dma((4,)),
            dma((2, 2)),
            dma((2, 2)),
            dma((2,)),
            dma((2,)),
        ],
        compiler_params=pltpu.CompilerParams(
            collective_id=0, has_side_effects=True, vmem_limit_bytes=56 * 2**20
        ),
    )(
        x0.reshape(act),
        w_key[0],
        w_value[0],
        w_score.reshape(1, model),
        segments,
        lengths.reshape(1, micro),
        grades,
    )
    grad_key, grad_value = pl.pallas_call(
        finish_kernel,
        out_shape=[jax.ShapeDtypeStruct((1, share, features), F32)] * 2,
        in_specs=[vmem] * 2,
        out_specs=[vmem] * 2,
    )(grad_key, grad_value)
    return (grad_key, grad_value)


def solution(mesh):
    placed = (
        P(None, "dp", None),
        P("section", None, None),
        P("section", None, None),
        P(),
        P(None, "dp"),
        P(None, "dp"),
        P(None, "dp"),
    )
    return jax.shard_map(
        shards,
        mesh=mesh,
        in_specs=placed,
        out_specs=(P("section", "dp", None), P("section", "dp", None)),
        check_vma=False,
    )
```
